128 devices in a mesh: gx: 32 (over y, z_hi, x), gy: 4 (over z_lo, core).
Axes of the slice: x: 4, y: 4, z: 4 (z_hi: 2, z_lo: 2; z = z_hi * 2 + z_lo), core: 2. Of those that a mesh axis runs over, the one named last changes fastest.
Arguments:
- permeability: float32 [10, 1024, 512], P(None, 'gx', 'gy'), may hold values from 0.1 to 10
- storage: float32 [10, 1024, 512], P(None, 'gx', 'gy'), may hold values from 0.02 to 0.5
- active_mask: int32 [1024, 512], P('gx', 'gy'), may hold values 0 or 1
- colour: int32 [10, 1024, 512], P(None, 'gx', 'gy'), may hold values from 0 to 1
- restrict_weight: float32 [10, 1024, 512], P(None, 'gx', 'gy'), may hold values from 0.5 to 1.5
- sweeps: int32 [4], replicated, may hold values from 1 to 3, as said below
- aggregate_map: int32 [128, 512], P('gx', 'gy'), may hold values from 0 to 511, as said below
- source_term: float32 [10, 1024, 512], P(None, 'gx', 'gy'), may hold values from -6 to 6
Outputs:
- solution_field: float32 [10, 1024, 512], P(None, 'gx', 'gy')
- final_residual: float32 [10, 1024, 512], P(None, 'gx', 'gy')
The draws below stay inside these ranges and needn't reach their ends.
Inputs may be any that keep to these rules, and one draw needn't show every extreme that they name: 3 sweeps on at least one level. `aggregate_map`: every aggregate holds some columns in every layer.
All inputs are finite; a program needn't handle non-finite values. No bound on the sum of `active_mask` on one device may be relied on, other than what follows from the above.
Results may differ from the reference program's by a relative error of at most 0.0003.
Values sent between devices are 32-bit elements; how exact they have to be, the bound alone decides.
A program may use at most 192 MiB of HBM per device.

```python
import math
import jax
import jax.numpy as jnp
from jax import lax

NZ = 10
LEVELS = 4
MAXSW = 3
NX = 1024
NY = 512
NXC = 128
NAGG = 512


def draw_colour(key, part):
    key = jax.random.fold_in(key, 11)
    flipped = jax.random.randint(key, (1, NX, NY), 0, 8)
    layer_idx = lax.broadcasted_iota(jnp.int32, (NZ, NX, NY), 0)
    column_x = lax.broadcasted_iota(jnp.int32, (NZ, NX, NY), 1)
    column_y = lax.broadcasted_iota(jnp.int32, (NZ, NX, NY), 2)
    return ((layer_idx + column_x + column_y + (flipped == 0).astype(jnp.int32)) % 2).astype(jnp.int32)


def draw_sweeps(key, part):
    key = jax.random.fold_in(key, 5)
    counts = jax.random.randint(key, (LEVELS,), 1, MAXSW + 1)
    chosen = jax.random.randint(jax.random.fold_in(key, 1), (), 0, LEVELS)
    return jnp.where(jnp.arange(LEVELS) == chosen, MAXSW, counts).astype(jnp.int32)


def draw_aggregate_map(key, part):
    key = jax.random.fold_in(key, 17)
    order = jax.random.permutation(key, NXC * NY).astype(jnp.int32)
    return (order % NAGG).reshape(NXC, NY).astype(jnp.int32)


def with_ends(values, stream_key, low, top_value):
    spot = [jax.random.randint(jax.random.fold_in(stream_key, axis), (), 0, length) for axis, length in enumerate(values.shape)]
    main_axis = values.shape.index(max(values.shape))
    next_to = spot[:main_axis] + [(spot[main_axis] + 1) % values.shape[main_axis]] + spot[main_axis + 1:]
    return values.at[tuple(spot)].set(low).at[tuple(next_to)].set(top_value)


def block_scale(key, dims, pieces, low, high):
    loudness, own = 1.0, jax.random.fold_in(key, 6)
    for axis_at, parts in pieces:
        heights = jnp.exp(jax.random.uniform(jax.random.fold_in(own, axis_at), (parts,), jnp.float32, low / len(pieces), high / len(pieces)))
        loudness = loudness * jnp.repeat(heights, dims[axis_at] // parts).reshape([-1 if axis == axis_at else 1 for axis in range(len(dims))])
    return loudness


def scatter_about(stream_key, shape, width, bound, cuts=(), dtype=jnp.bfloat16):
    factor_of = block_scale(stream_key, shape, cuts, -0.22, 0.18) if cuts else 1.0
    values = jax.random.normal(stream_key, shape, jnp.float32) * width * factor_of
    return jnp.minimum(jnp.maximum(values, -bound), bound).astype(dtype)


def setup_inputs(seed: int = 0) -> dict:
    seeds = jax.random.split(jax.random.key(seed), 9)
    return {
        "permeability": jnp.clip(jnp.exp(math.log(10.0) - 4.6051702 * jax.random.uniform(seeds[0], (NZ, NX, NY), jnp.float32) ** block_scale(seeds[0], (NZ, NX, NY), ((1, 32), (2, 4)), -0.2, 0.2)), 0.1, 10.0),
        "storage": jnp.clip(jnp.exp(math.log(0.5) - 3.218876 * jax.random.uniform(seeds[1], (NZ, NX, NY), jnp.float32) ** block_scale(seeds[1], (NZ, NX, NY), ((1, 32), (2, 4)), -0.2, 0.2)), 0.02, 0.5),
        "active_mask": with_ends((jax.random.randint(seeds[2], (NX, NY), 0, 8) < 7).astype(jnp.int32), jax.random.fold_in(seeds[2], 1), 0, 1),
        "colour": draw_colour(jax.random.fold_in(seeds[8], 71), 0),
        "restrict_weight": jnp.clip(0.5 + 1.0 * jax.random.uniform(seeds[4], (NZ, NX, NY), jnp.float32) ** block_scale(seeds[4], (NZ, NX, NY), ((1, 32), (2, 4)), -0.2, 0.2), 0.5, 1.5),
        "sweeps": draw_sweeps(jax.random.fold_in(seeds[8], 71), 0),
        "aggregate_map": draw_aggregate_map(jax.random.fold_in(seeds[8], 71), 0),
        "source_term": scatter_about(seeds[7], (NZ, NX, NY), 1.0, 6.0, ((1, 32), (2, 4)), jnp.float32),
    }


vertical_ratio = 0.5


def harmonic(first_value, second_value):
    return 2.0 * first_value * second_value / (first_value + second_value)


def build_level(perm_padded, act_padded, storage, colour):
    centre_perm = perm_padded[:, 1:-1, 1:-1]
    centre_act = act_padded[:, 1:-1, 1:-1]

    def face_term(other_perm, other_act):
        return harmonic(centre_perm, other_perm) * centre_act * other_act

    west_face = face_term(perm_padded[:, :-2, 1:-1], act_padded[:, :-2, 1:-1])
    east_face = face_term(perm_padded[:, 2:, 1:-1], act_padded[:, 2:, 1:-1])
    south_face = face_term(perm_padded[:, 1:-1, :-2], act_padded[:, 1:-1, :-2])
    north_face = face_term(perm_padded[:, 1:-1, 2:], act_padded[:, 1:-1, 2:])
    layered = jnp.pad(centre_perm, ((1, 1), (0, 0), (0, 0)))
    below_face = vertical_ratio * harmonic(centre_perm, layered[:-2]) * centre_act
    above_face = vertical_ratio * harmonic(centre_perm, layered[2:]) * centre_act
    diagonal_sum = storage + west_face + east_face + south_face + north_face + below_face + above_face
    centre = jnp.where(centre_act > 0, diagonal_sum, 1.0)
    return (centre, west_face, east_face, south_face, north_face, below_face, above_face, colour)


def coarsen(level):
    centre, west_face, east_face, south_face, north_face, below_face, above_face, colour = level
    return (centre[:, 0::2] + centre[:, 1::2] - 2.0 * east_face[:, 0::2], west_face[:, 0::2], east_face[:, 1::2],
            south_face[:, 0::2] + south_face[:, 1::2], north_face[:, 0::2] + north_face[:, 1::2],
            below_face[:, 0::2] + below_face[:, 1::2], above_face[:, 0::2] + above_face[:, 1::2], colour[:, 0::2])


def neighbours(level, padded):
    centre, west_face, east_face, south_face, north_face, below_face, above_face, colour = level
    middle = padded[:, 1:-1, 1:-1]
    layered = jnp.pad(middle, ((1, 1), (0, 0), (0, 0)))
    return (west_face * padded[:, :-2, 1:-1] + east_face * padded[:, 2:, 1:-1]
            + south_face * padded[:, 1:-1, :-2] + north_face * padded[:, 1:-1, 2:]
            + below_face * layered[:-2] + above_face * layered[2:])


def relax(level, padded, right_side, current, shade):
    updated = (right_side + neighbours(level, padded)) / level[0]
    return jnp.where(level[7] == shade, updated, current)


def zero_rim(values):
    return jnp.pad(values, ((0, 0), (1, 1), (1, 1)))


def residual(level, right_side, current):
    return right_side - (level[0] * current - neighbours(level, zero_rim(current)))


def aggregate_correction(centre, aggregate_map, leftover):
    flat_map = aggregate_map.reshape(-1).astype(jnp.int32)
    layers = leftover.shape[0]
    res_agg = jax.ops.segment_sum(leftover.reshape(layers, -1).T, flat_map, NAGG).T
    diag_agg = jax.ops.segment_sum(centre.reshape(layers, -1).T, flat_map, NAGG).T
    ratio = res_agg / diag_agg
    return jnp.take(ratio, flat_map, axis=1).reshape(leftover.shape)


def vcycle(levels, restrict_weight, sweeps, aggregate_map, start_rhs):
    deepest = len(levels) - 1

    def descend(depth, right_side):
        level = levels[depth]

        def sweep_once(step_index, current):
            current = relax(level, zero_rim(current), right_side, current, 0)
            return relax(level, zero_rim(current), right_side, current, 1)

        current = lax.fori_loop(0, sweeps[depth], sweep_once, jnp.zeros_like(right_side))
        leftover = residual(level, right_side, current)
        if depth == deepest:
            current = current + aggregate_correction(level[0], aggregate_map, leftover)
        else:
            if depth == 0:
                leftover = restrict_weight * leftover
            coarse_rhs = leftover[:, 0::2] + leftover[:, 1::2]
            current = current + jnp.repeat(descend(depth + 1, coarse_rhs), 2, axis=1)
        return lax.fori_loop(0, sweeps[depth], sweep_once, current)

    return descend(0, start_rhs)


def reference(permeability, storage, active_mask, colour, restrict_weight, sweeps, aggregate_map, source_term):
    act_full = jnp.broadcast_to(active_mask.astype(jnp.float32)[None], permeability.shape)
    level = build_level(zero_rim(permeability), zero_rim(act_full), storage, colour)
    levels = [level]
    for depth in range(LEVELS - 1):
        level = coarsen(level)
        levels.append(level)
    solution_field = vcycle(levels, restrict_weight, sweeps, aggregate_map, source_term)
    second_rhs = residual(levels[0], source_term, solution_field)
    solution_field = solution_field + vcycle(levels, restrict_weight, sweeps, aggregate_map, second_rhs)
    final_residual = residual(levels[0], source_term, solution_field)
    return solution_field, final_residual
```

```python
import functools
import jax
import jax.numpy as jnp
from jax import lax
from jax.experimental import pallas as pl
from jax.experimental.pallas import tpu as pltpu
from jax.sharding import PartitionSpec as P

MESH = pl.DeviceIdType.MESH
F32 = jnp.float32
NZ = 10
T2 = 2 * NZ
LEVELS = 4
NAGG = 512
ROWS = (6, 6, 4, 4)
HALO = (8, 16, 12, 12)
OWN = (32, 16, 8, 4)
LIN = (48, 48, 40, 32)
LO = (8, 16, 16, 12)
WS = (0, 0, 4, 0)
REACH = ((1, -1), (1, -1), (1, -1, 2, -2), (1, -1, 2, -2, 3, -3))
SO = 8
ST_ROWS = (48, 32, 24, 24)
ST_OFF = (0, 4, 0, 2)
ES_OFF = (0, 0, 4, 4)
ES_ROWS = (48, 48, 40, 40)
ARR = 24
ZC = 5

X_PARTNERS = ((1, 0), (2, 0), (3, 0))
Y_PARTNERS = ((8, 0), (16, 0), (24, 0))
Z_PARTNERS = ((4, 0), (0, 2), (4, 2))


def pads(buf, rows):
    buf[0] = pltpu.roll(buf[rows], 1, 1)
    buf[rows + 1] = pltpu.roll(buf[1], 7, 1)


def beside(own, other, shift, edge):
    moved, moved_other = pltpu.roll(own, shift, 2), pltpu.roll(other, shift, 2)
    return jnp.where(edge, moved_other, moved), jnp.where(edge, moved, moved_other)


def zshift(buf, row, values, tile, first, last, up):
    base = tile * NZ
    if up:
        tail = values[-1:] if last == NZ else buf[row, base + last : base + last + 1]
        return jnp.concatenate([values[1:], tail], axis=0) if last - first > 1 else tail
    head = values[:1] if first == 0 else buf[row, base + first - 1 : base + first]
    return jnp.concatenate([head, values[:-1]], axis=0) if last - first > 1 else head


def neighbour_sum(cf, src, i, first, last):
    lane = lax.broadcasted_iota(jnp.int32, (last - first, 8, 128), 2)
    span = [slice(t * NZ + first, t * NZ + last) for t in (0, 1)]
    own = [src[i + 1, span[t]] for t in (0, 1)]
    south = beside(own[0], own[1], 1, lane == 0)
    north = beside(own[0], own[1], 127, lane == 127)
    sums = []
    for t in (0, 1):
        acc = cf[i, 0, span[t]] * src[i, span[t]]
        acc += cf[i, 1, span[t]] * src[i + 2, span[t]]
        acc += cf[i, 4, span[t]] * zshift(src, i + 1, own[t], t, first, last, False)
        acc += cf[i, 5, span[t]] * zshift(src, i + 1, own[t], t, first, last, True)
        acc += cf[i, 2, span[t]] * south[t]
        acc += cf[i, 3, span[t]] * north[t]
        sums.append(acc)
    return span, own, sums


def kernel(
    gxn,
    gyn,
    perm,
    stor,
    act,
    colour,
    rweight,
    sweeps,
    amap,
    source,
    sol,
    fres,
    y0,
    yl,
    yr,
    f0,
    rw,
    raw,
    cfs,
    ccs,
    cis,
    cols,
    rps,
    eas,
    ebs,
    ks,
    kw,
    sts,
    lrs,
    ess,
    els,
    cls,
    idx,
    onehot,
    agg,
    ar_keep,
    ar_give,
    ar_core,
    ar_sum,
    ar_in,
    ar_last,
    ratio,
    wlin,
    send,
    recv,
):
    gx, gy = lax.axis_index("gx"), lax.axis_index("gy")
    core = lax.rem(gy, 2)

    def ring(dx, dy):
        return (lax.rem(gx + dx + gxn, gxn), lax.rem(gy + dy + gyn, gyn))

    def flip(dx, dy):
        return (jnp.bitwise_xor(gx, dx), jnp.bitwise_xor(gy, dy))

    counter = [0]

    def sems(n):
        counter[0] += n
        return counter[0] - n

    def copy(src, dst, sem, device):
        return pltpu.make_async_remote_copy(
            src_ref=src, dst_ref=dst, send_sem=send.at[sem], recv_sem=recv.at[sem],
            device_id=device, device_id_type=MESH,
        )

    def start(copies):
        for c in copies:
            c.start()

    def finish(copies):
        for c in copies:
            c.wait()

    barrier = pltpu.get_barrier_semaphore()
    partners = [ring(d, 0) for d in REACH[3]] + [ring(0, 1), ring(0, -1)]
    partners += [flip(*p) for p in X_PARTNERS + Y_PARTNERS + Z_PARTNERS + ((0, 1),)]
    for device in partners:
        pl.semaphore_signal(barrier, inc=1, device_id=device, device_id_type=MESH)

    active = act[...] > 0
    for z in range(NZ):
        y0[z] = jnp.where(active, perm[z], 0.0)
        y0[NZ + z] = jnp.where(active, stor[z], 1.0)
        y0[2 * NZ + z] = colour[z].astype(F32)
        y0[3 * NZ + z] = source[z]
        y0[4 * NZ + z] = rweight[z]
    y0[50, 0:4] = amap[...].astype(F32)
    pl.semaphore_wait(barrier, len(partners))

    s_y = sems(2)
    s_x = sems(2)

    def y_copies(span):
        return [
            copy(y0.at[span], yl.at[span], s_y, ring(0, 1)),
            copy(y0.at[span], yr.at[span], s_y + 1, ring(0, -1)),
        ]

    def x_copies(span, buf, base):
        return [
            copy(buf.at[span, :, 32:40], buf.at[span, :, 0:8], base, ring(1, 0)),
            copy(buf.at[span, :, 8:16], buf.at[span, :, 40:48], base + 1, ring(-1, 0)),
        ]

    def join(k):
        lane = lax.broadcasted_iota(jnp.int32, (NZ, 32, 128), 2)
        part = slice(k * NZ, k * NZ + NZ)
        return y0[part], jnp.where(lane < 64, yr[part], yl[part])

    everything = slice(0, 51)
    start(y_copies(everything))
    for j in range(4):
        agg_id = lax.broadcasted_iota(jnp.int32, (NAGG, 128), 0)
        onehot[j] = (agg_id == amap[j : j + 1, :]).astype(jnp.bfloat16)
    agg[...] = jnp.zeros_like(agg)
    finish(y_copies(everything))
    for k in range(4):
        mine, other = join(k)
        f0[k, 0:NZ, 8:40] = mine
        f0[k, NZ:T2, 8:40] = other
    wlin[...] = jnp.zeros_like(wlin)
    mine, other = join(4)
    wlin[0:NZ, 8:40] = mine
    wlin[NZ:T2, 8:40] = other
    start(x_copies(slice(0, 4), f0, s_x))
    for i in range(6):
        rw[i] = wlin[:, pl.ds(i, 8, stride=6), :]
    mlane = lax.broadcasted_iota(jnp.int32, (4, 128), 1)
    ks[3][100, 8:12] = y0[50, 0:4]
    ks[3][101, 8:12] = jnp.where(mlane < 64, yr[50, 0:4], yl[50, 0:4])
    finish(x_copies(slice(0, 4), f0, s_x))

    ea0 = eas[0]
    for i in range(6):
        ea0[i + 1] = f0[0, :, pl.ds(i, 8, stride=6), :]
    pads(ea0, 6)
    lane = lax.broadcasted_iota(jnp.int32, (NZ, 8, 128), 2)
    sub = lax.broadcasted_iota(jnp.int32, (NZ, 8, 128), 1)
    layer = lax.broadcasted_iota(jnp.int32, (NZ, 8, 128), 0)

    def harmonic(a, b):
        total = a + b
        return jnp.where(total > 0, 2.0 * a * b / jnp.where(total > 0, total, 1.0), 0.0)

    def faces0(i, carry):
        own = [ea0[i + 1, t * NZ : t * NZ + NZ] for t in (0, 1)]
        north = beside(own[0], own[1], 127, lane == 127)
        xg = gx * 32 - 8 + 6 * sub + i
        for t in (0, 1):
            part = slice(t * NZ, t * NZ + NZ)
            west = harmonic(own[t], ea0[i, part])
            yg = gy * 128 + lane
            if t == 1:
                yg = jnp.where(lane < 64, yg + 128, yg - 128)
            raw[0, i, part] = jnp.where((xg == 0) | (xg == 1024), 0.0, west)
            raw[1, i, part] = jnp.where(jnp.bitwise_and(yg, 511) == 511, 0.0, harmonic(own[t], north[t]))
            above = 0.5 * harmonic(own[t], zshift(ea0, i + 1, own[t], t, 0, NZ, True))
            raw[2, i, part] = jnp.where(layer == NZ - 1, 0.0, above)
        return carry

    lax.fori_loop(0, 6, faces0, 0)

    def scaled(l, storage_of, west_of, north_of, above_of, colour_of):
        rows, pad = ROWS[l], eas[l]
        for i in range(rows):
            pad[i + 1] = west_of(i)
        pads(pad, rows)
        for i in range(rows):
            north, above = north_of(i), above_of(i)
            south = beside(north[0:NZ], north[NZ:T2], 1, lane == 0)
            zero = jnp.zeros((1, 8, 128), F32)
            below = [
                jnp.concatenate([zero, above[t * NZ : t * NZ + NZ - 1]], axis=0) for t in (0, 1)
            ]
            storage, shade = storage_of(i), colour_of(i)
            for t in (0, 1):
                part = slice(t * NZ, t * NZ + NZ)
                west, east = pad[i + 1, part], pad[i + 2, part]
                six = (west, east, south[t], north[part], below[t], above[part])
                centre = storage[part] + west + east + south[t] + north[part] + below[t] + above[part]
                inverse = 1.0 / centre
                for k in range(6):
                    cfs[l][i, k, part] = six[k] * inverse
                ccs[l][i, part] = centre
                cis[l][i, part] = inverse
                cols[l][i, part] = shade[part]

    def pick0(k):
        return lambda i: f0[k, :, pl.ds(i, 8, stride=6), :]

    scaled(0, pick0(1), lambda i: raw[0, i], lambda i: raw[1, i], lambda i: raw[2, i], pick0(2))

    for m in range(3):
        even, odd = 2 * m, 2 * m + 1
        five = (
            f0[1, :, pl.ds(even, 8, stride=6), :] + f0[1, :, pl.ds(odd, 8, stride=6), :],
            raw[0, even],
            raw[1, even] + raw[1, odd],
            raw[2, even] + raw[2, odd],
            f0[2, :, pl.ds(even, 8, stride=6), :],
        )
        for k in range(5):
            ks[1][k * T2 : k * T2 + T2, pl.ds(4 + m, 8, stride=3), :] = five[k]
    for l in (2, 3):
        for k in range(5):
            part = slice(k * T2, k * T2 + T2)
            value = ks[l - 1][part, pl.ds(8, 8, stride=2), :]
            if k not in (1, 4):
                value = value + ks[l - 1][part, pl.ds(9, 8, stride=2), :]
            ks[l][part, 8:16] = value

    s_k = [None] + [sems(len(REACH[l])) for l in (1, 2, 3)]
    s_r = [None] + [sems(len(REACH[l])) for l in (1, 2, 3)]
    s_e = [sems(len(REACH[l])) for l in range(4)]
    s_ar = sems(22)

    def spread_copies(l, src, src_at, dst, base):
        n = OWN[l]
        return [
            copy(
                src.at[:, src_at : src_at + n],
                dst.at[:, LO[l] - n * d : LO[l] - n * d + n],
                base + k,
                ring(d, 0),
            )
            for k, d in enumerate(REACH[l])
        ]

    def keep_own(l, src, src_at, dst):
        n = OWN[l]
        dst[:, LO[l] : LO[l] + n] = src[:, src_at : src_at + n]
        if l == 3:
            dst[:, 28:32] = src[:, src_at : src_at + n]

    def k_copies(l):
        return spread_copies(l, ks[l], SO, kw[l], s_k[l])

    def level_coefficients(l):
        keep_own(l, ks[l], SO, kw[l])
        finish(k_copies(l))

        def pick(k):
            return lambda i: kw[l][
                k * T2 : k * T2 + T2, pl.ds(WS[l] + i, 8, stride=ROWS[l]), :
            ]

        scaled(l, pick(0), pick(1), pick(2), pick(3), pick(4))

    def half(l, src, dst, shade):
        def row(i, carry):
            for first in range(0, NZ, ZC):
                span, own, sums = neighbour_sum(cfs[l], src, i, first, first + ZC)
                for t in (0, 1):
                    fresh = rps[l][i, span[t]] + sums[t]
                    dst[i + 1, span[t]] = jnp.where(cols[l][i, span[t]] == shade, fresh, own[t])
            return carry

        lax.fori_loop(0, ROWS[l], row, 0)
        pads(dst, ROWS[l])

    def left_over(l, src, i, first, last):
        span, own, sums = neighbour_sum(cfs[l], src, i, first, last)
        return span, [
            ccs[l][i, span[t]] * (rps[l][i, span[t]] + sums[t] - own[t]) for t in (0, 1)
        ]

    def before(l, lin):
        ea, eb = eas[l], ebs[l]
        for i in range(ROWS[l]):
            scaled_rhs = lin[:, pl.ds(WS[l] + i, 8, stride=ROWS[l]), :] * cis[l][i]
            rps[l][i] = scaled_rhs
            ea[i + 1] = jnp.where(cols[l][i] == 0.0, scaled_rhs, 0.0)
        pads(ea, ROWS[l])
        half(l, ea, eb, 1.0)

        def sweep(j, carry):
            on = j < sweeps[l]
            half(l, eb, ea, jnp.where(on, 0.0, -1.0))
            half(l, ea, eb, jnp.where(on, 1.0, -1.0))
            return carry

        lax.fori_loop(1, 3, sweep, 0)

    def after(l):
        ea, eb = eas[l], ebs[l]

        def sweep(j, carry):
            on = j < sweeps[l]
            half(l, ea, eb, jnp.where(on, 0.0, -1.0))
            half(l, eb, ea, jnp.where(on, 1.0, -1.0))
            return carry

        lax.fori_loop(0, 3, sweep, 0)

    def restrict(l):
        stage, rows = sts[l + 1], ROWS[l] // 2

        for m in range(rows):
            for first in range(0, NZ, ZC):
                total = None
                for i in (2 * m, 2 * m + 1):
                    span, res = left_over(l, ebs[l], i, first, first + ZC)
                    if l == 0:
                        res = [rw[i, span[t]] * res[t] for t in (0, 1)]
                    total = res if total is None else [total[t] + res[t] for t in (0, 1)]
                for t in (0, 1):
                    stage[span[t], pl.ds(ST_OFF[l + 1] + m, 8, stride=rows), :] = total[t]

    def stage_iterate(l):
        for i in range(ROWS[l]):
            ess[l][:, pl.ds(ES_OFF[l] + i, 8, stride=ROWS[l]), :] = ebs[l][i + 1]

    def r_copies(l):
        return spread_copies(l, sts[l], SO, lrs[l], s_r[l])

    def e_copies(l):
        own_at = ES_OFF[l] + HALO[l]
        if l == 0:
            return [
                copy(ess[0].at[:, 32:40], els[0].at[:, 0:8], s_e[0], ring(1, 0)),
                copy(ess[0].at[:, 8:16], els[0].at[:, 40:48], s_e[0] + 1, ring(-1, 0)),
            ]
        return spread_copies(l, ess[l], own_at, els[l], s_e[l])

    def aggregate_ratio(cyc):
        s_a = s_ar + cyc * 11
        for first in range(0, NZ, ZC):
            for i in range(4):
                span, res = left_over(3, ebs[3], i, first, first + ZC)
                wlin[span[0], pl.ds(i, 8, stride=4), :] = res[0]
        for i in range(4):
            wlin[NZ:T2, pl.ds(i, 8, stride=4), :] = ccs[3][i, 0:NZ]
        total = jnp.zeros((3 * ARR, NAGG), F32)
        for i in range(4):
            for z in range(T2):
                agg[z : z + 1] = wlin[z, 12 + i : 13 + i, :]
            value = agg[...]
            high = value.astype(jnp.bfloat16)
            rest = value - high.astype(F32)
            middle = rest.astype(jnp.bfloat16)
            low = (rest - middle.astype(F32)).astype(jnp.bfloat16)
            three = jnp.concatenate([high.astype(F32), middle.astype(F32), low.astype(F32)], axis=0)
            total += lax.dot_general(
                three.astype(jnp.bfloat16), onehot[i], (((1,), (1,)), ((), ())),
                preferred_element_type=F32,
            )
        mine = total[0:ARR] + total[ARR : 2 * ARR] + total[2 * ARR :]
        low_half, high_half = mine[:, 0:256], mine[:, 256:512]
        ar_keep[...] = jnp.where(core == 0, low_half, high_half)
        ar_give[...] = jnp.where(core == 0, high_half, low_half)
        first_copy = copy(ar_give, ar_core.at[cyc], s_a, flip(0, 1))
        first_copy.start()
        stage_iterate(3)
        first_copy.wait()
        ar_sum[0] = ar_keep[...] + ar_core[cyc]
        at = 1
        for stage, group in enumerate((X_PARTNERS, Y_PARTNERS, Z_PARTNERS)):
            copies = [
                copy(ar_sum.at[stage], ar_in.at[cyc, stage, k], s_a + at + k, flip(*p))
                for k, p in enumerate(group)
            ]
            start(copies)
            if stage == 0:
                for l in (3, 2, 1, 0):
                    start(e_copies(l))
                for l in range(4):
                    own_at = ES_OFF[l] + HALO[l]
                    els[l][:, LO[l] : LO[l] + OWN[l]] = ess[l][:, own_at : own_at + OWN[l]]
                els[3][:, 28:32] = ess[3][:, 16:20]
            finish(copies)
            ar_sum[stage + 1] = ar_sum[stage] + ar_in[cyc, stage, 0] + ar_in[cyc, stage, 1] + ar_in[cyc, stage, 2]
            at += 3
        last_copy = copy(ar_sum.at[3], ar_last.at[cyc], s_a + 10, flip(0, 1))
        last_copy.start()
        last_copy.wait()
        mine, other = ar_sum[3], ar_last[cyc]
        low_half = jnp.where(core == 0, mine, other)
        high_half = jnp.where(core == 0, other, mine)
        ratio[0:NZ, 0:256] = low_half[0:NZ] / low_half[NZ:T2]
        ratio[0:NZ, 256:512] = high_half[0:NZ] / high_half[NZ:T2]

    def window_iterate(l):
        finish(e_copies(l))
        for i in range(ROWS[l]):
            now = els[l][:, pl.ds(WS[l] + i, 8, stride=ROWS[l]), :]
            if l < 3:
                at = HALO[l + 1] - HALO[l] // 2 + i // 2
                now = now + cls[l + 1][:, pl.ds(at, 8, stride=ROWS[l] // 2), :]
            eas[l][i + 1] = now

    def add_aggregates():
        def row(i, carry):
            for t in (0, 1):
                where = idx[i, t]
                place, block = jnp.bitwise_and(where, 127), jnp.right_shift(where, 7)
                for z in range(NZ):
                    value = jnp.zeros((8, 128), F32)
                    for k in range(4):
                        table = jnp.broadcast_to(
                            ratio[z : z + 1, 128 * k : 128 * k + 128], (8, 128)
                        )
                        found = jnp.take_along_axis(table, place, axis=1)
                        value = jnp.where(block == k, found, value)
                    eas[3][i + 1, t * NZ + z] += value
            return carry

        lax.fori_loop(0, 4, row, 0)

    def cycle(cyc, carry):
        first = cyc == 0
        for l in range(4):
            before(l, f0.at[3] if l == 0 else lrs[l])
            if l < 3:
                restrict(l)
                start(r_copies(l + 1))

                @pl.when(first)
                def _():
                    if l == 0:
                        start(k_copies(1))
                    level_coefficients(l + 1)
                    if l + 1 < 3:
                        start(k_copies(l + 2))
                    else:
                        for i in range(4):
                            for t in (0, 1):
                                found = kw[3][100 + t, pl.ds(i, 8, stride=4), :]
                                idx[i, t] = found.astype(jnp.int32)

                stage_iterate(l)
                keep_own(l + 1, sts[l + 1], SO, lrs[l + 1])
                finish(r_copies(l + 1))
        aggregate_ratio(cyc)
        for l in (3, 2, 1, 0):
            window_iterate(l)
            if l == 3:
                add_aggregates()
            pads(eas[l], ROWS[l])
            after(l)
            if l > 0:
                for i in range(ROWS[l]):
                    cls[l][:, pl.ds(i, 8, stride=ROWS[l]), :] = eas[l][i + 1]

        for i in range(6):
            wlin[0:NZ, pl.ds(i, 8, stride=6), :] = eas[0][i + 1, 0:NZ]
        added = wlin[0:NZ, 8:40]

        @pl.when(first)
        def _():
            sol[...] = added

        @pl.when(jnp.logical_not(first))
        def _():
            sol[...] += added

        for i in range(6):
            for z in range(0, NZ, ZC):
                span, res = left_over(0, eas[0], i, z, z + ZC)
                wlin[span[0], pl.ds(i, 8, stride=6), :] = res[0]
        leftover = wlin[0:NZ, 8:40]

        @pl.when(first)
        def _():
            part = slice(3 * NZ, 4 * NZ)
            y0[part] = leftover
            start(y_copies(part))
            finish(y_copies(part))
            mine, other = join(3)
            f0[3, 0:NZ, 8:40] = mine
            f0[3, NZ:T2, 8:40] = other
            start(x_copies(slice(3, 4), f0, s_x))
            finish(x_copies(slice(3, 4), f0, s_x))

        @pl.when(jnp.logical_not(first))
        def _():
            fres[...] = leftover

        return carry

    lax.fori_loop(0, 2, cycle, 0)


def on_device(gxn, gyn, perm, stor, act, colour, rweight, sweeps, amap, source):
    def vm(*shape, dtype=F32):
        return pltpu.VMEM(shape, dtype)

    levels = range(LEVELS)
    scratch = [
        vm(51, 32, 128),
        vm(51, 32, 128),
        vm(51, 32, 128),
        vm(4, T2, 48, 128),
        vm(6, T2, 8, 128),
        vm(3, 6, T2, 8, 128),
        [vm(ROWS[l], 6, T2, 8, 128) for l in levels],
        [vm(ROWS[l], T2, 8, 128) for l in levels],
        [vm(ROWS[l], T2, 8, 128) for l in levels],
        [vm(ROWS[l], T2, 8, 128) for l in levels],
        [vm(ROWS[l], T2, 8, 128) for l in levels],
        [vm(ROWS[l] + 2, T2, 8, 128) for l in levels],
        [vm(ROWS[l] + 2, T2, 8, 128) for l in levels],
        [vm(102 if l == 3 else 100, ST_ROWS[l], 128) for l in levels],
        [vm(102 if l == 3 else 100, LIN[l], 128) for l in levels],
        [vm(T2, ST_ROWS[l], 128) for l in levels],
        [vm(T2, LIN[l], 128) for l in levels],
        [vm(T2, ES_ROWS[l], 128) for l in levels],
        [vm(T2, LIN[l], 128) for l in levels],
        [vm(T2, 8 * ROWS[l], 128) for l in levels],
        vm(4, 2, 8, 128, dtype=jnp.int32),
        vm(4, NAGG, 128, dtype=jnp.bfloat16),
        vm(ARR, 128),
        vm(ARR, 256),
        vm(ARR, 256),
        vm(2, ARR, 256),
        vm(4, ARR, 256),
        vm(2, 3, 3, ARR, 256),
        vm(2, ARR, 256),
        vm(16, NAGG),
        vm(T2, 48, 128),
        pltpu.SemaphoreType.DMA((64,)),
        pltpu.SemaphoreType.DMA((64,)),
    ]
    vmem = pl.BlockSpec(memory_space=pltpu.VMEM)
    smem = pl.BlockSpec(memory_space=pltpu.SMEM)
    out = jax.ShapeDtypeStruct(perm.shape, F32)
    return pl.pallas_call(
        functools.partial(kernel, gxn, gyn),
        out_shape=(out, out),
        in_specs=[vmem, vmem, vmem, vmem, vmem, smem, vmem, vmem],
        out_specs=(vmem, vmem),
        scratch_shapes=scratch,
        compiler_params=pltpu.CompilerParams(
            collective_id=0, has_side_effects=True, vmem_limit_bytes=60 * 2**20
        ),
    )(perm, stor, act, colour, rweight, sweeps, amap, source)


def solution(mesh):
    field = P(None, "gx", "gy")
    column = P("gx", "gy")
    return jax.shard_map(
        functools.partial(on_device, mesh.shape["gx"], mesh.shape["gy"]),
        mesh=mesh,
        in_specs=(field, field, column, field, field, P(), column, field),
        out_specs=(field, field),
        check_vma=False,
    )
```

```python
import functools
import jax
import jax.numpy as jnp
from jax import lax
from jax.experimental import pallas as pl
from jax.experimental.pallas import tpu as pltpu
from jax.sharding import PartitionSpec as P

MESH = pl.DeviceIdType.MESH
F32 = jnp.float32
NZ = 10
T2 = 2 * NZ
LEVELS = 4
NAGG = 512
ROWS = (6, 6, 4, 4)
HALO = (8, 16, 12, 12)
OWN = (32, 16, 8, 4)
LIN = (48, 48, 40, 32)
LO = (8, 16, 16, 12)
WS = (0, 0, 4, 0)
NEAR = (
    (),
    ((1, 8, 16, 8, 16), (-1, 0, 8, 32, 40)),
    ((1, 0, 8, 8, 16), (-1, 0, 8, 24, 32)),
    ((1, 0, 4, 8, 12), (-1, 0, 4, 16, 20), (2, 0, 4, 4, 8), (-2, 0, 4, 20, 24)),
)
FAR = (
    (),
    ((1, 4, 8, 4, 8), (-1, 8, 12, 40, 44)),
    ((2, 4, 8, 4, 8), (-2, 0, 4, 32, 36)),
    ((3, 0, 4, 0, 4), (-3, 0, 4, 24, 28)),
)
ITERATE = (
    ((1, 24, 32, 0, 8), (-1, 0, 8, 40, 48)),
    ((1, 4, 16, 4, 16), (-1, 0, 12, 32, 44)),
    NEAR[2] + FAR[2],
    NEAR[3] + FAR[3],
)
SO = 8
ST_ROWS = (48, 32, 24, 24)
ST_OFF = (0, 4, 0, 2)
ES_OFF = (0, 0, 4, 4)
ES_ROWS = (48, 48, 40, 40)
ARR = 24
ZC = 2

X_PARTNERS = ((1, 0), (2, 0), (3, 0))
Y_PARTNERS = ((8, 0), (16, 0), (24, 0))
Z_PARTNERS = ((4, 0), (0, 2), (4, 2))


def pads(buf, rows):
    buf[0] = pltpu.roll(buf[rows], 1, 1)
    buf[rows + 1] = pltpu.roll(buf[1], 7, 1)


def beside(own, other, shift, edge):
    moved, moved_other = pltpu.roll(own, shift, 2), pltpu.roll(other, shift, 2)
    return jnp.where(edge, moved_other, moved), jnp.where(edge, moved, moved_other)


def zshift(buf, row, values, tile, first, last, up):
    base = tile * NZ
    if up:
        tail = values[-1:] if last == NZ else buf[row, base + last : base + last + 1]
        return jnp.concatenate([values[1:], tail], axis=0) if last - first > 1 else tail
    head = values[:1] if first == 0 else buf[row, base + first - 1 : base + first]
    return jnp.concatenate([head, values[:-1]], axis=0) if last - first > 1 else head


def neighbour_sum(cf, src, i, first, last):
    lane = lax.broadcasted_iota(jnp.int32, (last - first, 8, 128), 2)
    span = [slice(t * NZ + first, t * NZ + last) for t in (0, 1)]
    own = [src[i + 1, span[t]] for t in (0, 1)]
    south = beside(own[0], own[1], 1, lane == 0)
    north = beside(own[0], own[1], 127, lane == 127)
    sums = []
    for t in (0, 1):
        acc = cf[i, 0, span[t]] * src[i, span[t]]
        acc += cf[i, 1, span[t]] * src[i + 2, span[t]]
        acc += cf[i, 4, span[t]] * zshift(src, i + 1, own[t], t, first, last, False)
        acc += cf[i, 5, span[t]] * zshift(src, i + 1, own[t], t, first, last, True)
        acc += cf[i, 2, span[t]] * south[t]
        acc += cf[i, 3, span[t]] * north[t]
        sums.append(acc)
    return span, own, sums


def kernel(
    gxn,
    gyn,
    perm,
    stor,
    act,
    colour,
    rweight,
    sweeps,
    amap,
    source,
    sol,
    fres,
    y0,
    yp,
    yn,
    f0,
    rw,
    raw,
    cfs,
    ccs,
    cis,
    cols,
    rps,
    eas,
    ebs,
    ks,
    kw,
    kf,
    sts,
    lrs,
    lrf,
    ess,
    els,
    cls,
    idx,
    onehot,
    agg,
    ar_keep,
    ar_give,
    ar_core,
    ar_sum,
    ar_in,
    ar_last,
    ratio,
    wlin,
    send,
    recv,
):
    gx, gy = lax.axis_index("gx"), lax.axis_index("gy")
    core = lax.rem(gy, 2)

    def ring(dx, dy):
        return (lax.rem(gx + dx + gxn, gxn), lax.rem(gy + dy + gyn, gyn))

    def flip(dx, dy):
        return (jnp.bitwise_xor(gx, dx), jnp.bitwise_xor(gy, dy))

    counter = [0]

    def sems(n):
        counter[0] += n
        return counter[0] - n

    def copy(src, dst, sem, device):
        return pltpu.make_async_remote_copy(
            src_ref=src, dst_ref=dst, send_sem=send.at[sem], recv_sem=recv.at[sem],
            device_id=device, device_id_type=MESH,
        )

    def start(copies):
        for c in copies:
            c.start()

    def finish(copies):
        for c in copies:
            c.wait()

    barrier = pltpu.get_barrier_semaphore()
    partners = [ring(d, 0) for d in (1, -1, 2, -2, 3, -3)] + [ring(0, 1), ring(0, -1)]
    partners += [flip(*p) for p in X_PARTNERS + Y_PARTNERS + Z_PARTNERS + ((0, 1),)]
    for device in partners:
        pl.semaphore_signal(barrier, inc=1, device_id=device, device_id_type=MESH)

    active = act[...] > 0
    for z in range(NZ):
        y0[z] = jnp.where(active, perm[z], 0.0)
        y0[NZ + z] = jnp.where(active, stor[z], 1.0)
        y0[2 * NZ + z] = colour[z].astype(F32)
        y0[3 * NZ + z] = source[z]
        y0[4 * NZ + z] = rweight[z]
    own_map = amap[...].astype(F32)

    s_y = sems(2)
    s_x = sems(2)

    lane10 = lax.broadcasted_iota(jnp.int32, (NZ, 16, 128), 2)

    def pack(k):
        part = slice(k * NZ, k * NZ + NZ)
        upper, lower = y0[part, 0:16], y0[part, 16:32]
        yp[0, part] = jnp.where(lane10 < 64, pltpu.roll(upper, 64, 2), lower)
        yp[1, part] = jnp.where(lane10 < 64, upper, pltpu.roll(lower, 64, 2))

    def y_exchange(span, between):
        right = copy(yp.at[0, span], yn.at[0, span], s_y, ring(0, 1))
        left = copy(yp.at[1, span], yn.at[1, span], s_y + 1, ring(0, -1))

        @pl.when(gy < gyn - 1)
        def _():
            right.start()

        @pl.when(gy > 0)
        def _():
            left.start()

        @pl.when(gy == 0)
        def _():
            yn[0, span] = yp[0, span]

        @pl.when(gy == gyn - 1)
        def _():
            yn[1, span] = yp[1, span]

        between()

        @pl.when(gy < gyn - 1)
        def _():
            right.wait_send()
            left.wait_recv()

        @pl.when(gy > 0)
        def _():
            left.wait_send()
            right.wait_recv()

    def x_copies(span, buf, base):
        return [
            copy(buf.at[span, :, 32:40], buf.at[span, :, 0:8], base, ring(1, 0)),
            copy(buf.at[span, :, 8:16], buf.at[span, :, 40:48], base + 1, ring(-1, 0)),
        ]

    def join(k):
        part = slice(k * NZ, k * NZ + NZ)
        right, left = yn[1, part], yn[0, part]
        upper = jnp.where(lane10 < 64, right, pltpu.roll(left, 64, 2))
        lower = jnp.where(lane10 < 64, pltpu.roll(right, 64, 2), left)
        return upper, lower

    def fill_beside():
        for j in range(4):
            agg_id = lax.broadcasted_iota(jnp.int32, (NAGG, 128), 0)
            onehot[j] = (agg_id == amap[j : j + 1, :]).astype(jnp.bfloat16)
        agg[...] = jnp.zeros_like(agg)
        wlin[...] = jnp.zeros_like(wlin)
        for l in (1, 2, 3):
            lrs[l][...] = jnp.zeros_like(lrs[l])
            els[l][...] = jnp.zeros_like(els[l])
        for _, _, _, at, end in FAR[1] + ((0, 0, 0, 0, 4), (0, 0, 0, 44, 48)):
            kw[1][:, at:end] = jnp.ones((100, end - at, 128), F32)
        for l in (2, 3):
            for _, _, _, at, end in FAR[l]:
                kw[l][0:100, at:end] = jnp.ones((100, end - at, 128), F32)
        for _, _, _, at, end in FAR[3]:
            kw[3][100:102, at:end] = jnp.zeros((2, end - at, 128), F32)
        for k in range(4):
            f0[k, 0:NZ, 8:40] = y0[k * NZ : k * NZ + NZ]
        wlin[0:NZ, 8:40] = y0[4 * NZ : 5 * NZ]

    for k in range(5):
        pack(k)
    yp[0, 50, 0:4] = own_map
    yp[1, 50, 0:4] = own_map
    pl.semaphore_wait(barrier, len(partners))
    y_exchange(slice(0, 51), fill_beside)
    for k in range(4):
        upper, lower = join(k)
        f0[k, NZ:T2, 8:24] = upper
        f0[k, NZ:T2, 24:40] = lower
    upper, lower = join(4)
    wlin[NZ:T2, 8:24] = upper
    wlin[NZ:T2, 24:40] = lower
    start(x_copies(slice(0, 4), f0, s_x))
    for i in range(6):
        rw[i] = wlin[:, pl.ds(i, 8, stride=6), :]
    mlane = lax.broadcasted_iota(jnp.int32, (4, 128), 1)
    ks[3][100, 8:12] = own_map
    ks[3][101, 8:12] = jnp.where(mlane < 64, yn[1, 50, 0:4], yn[0, 50, 0:4])
    finish(x_copies(slice(0, 4), f0, s_x))

    ea0 = eas[0]
    for i in range(6):
        ea0[i + 1] = f0[0, :, pl.ds(i, 8, stride=6), :]
    pads(ea0, 6)
    lane = lax.broadcasted_iota(jnp.int32, (NZ, 8, 128), 2)
    sub = lax.broadcasted_iota(jnp.int32, (NZ, 8, 128), 1)
    layer = lax.broadcasted_iota(jnp.int32, (NZ, 8, 128), 0)

    def harmonic(a, b):
        total = a + b
        return jnp.where(total > 0, 2.0 * a * b / jnp.where(total > 0, total, 1.0), 0.0)

    for i in range(6):
        own = [ea0[i + 1, t * NZ : t * NZ + NZ] for t in (0, 1)]
        north = beside(own[0], own[1], 127, lane == 127)
        xg = gx * 32 - 8 + 6 * sub + i
        for t in (0, 1):
            part = slice(t * NZ, t * NZ + NZ)
            west = harmonic(own[t], ea0[i, part])
            yg = gy * 128 + lane
            if t == 1:
                yg = jnp.where(lane < 64, yg + 128, yg - 128)
            raw[0, i, part] = jnp.where((xg == 0) | (xg == 1024), 0.0, west)
            raw[1, i, part] = jnp.where(jnp.bitwise_and(yg, 511) == 511, 0.0, harmonic(own[t], north[t]))
            above = 0.5 * harmonic(own[t], zshift(ea0, i + 1, own[t], t, 0, NZ, True))
            raw[2, i, part] = jnp.where(layer == NZ - 1, 0.0, above)

    def scaled(l, storage_of, west_of, north_of, above_of, colour_of):
        rows, pad = ROWS[l], eas[l]
        for i in range(rows):
            pad[i + 1] = west_of(i)
        pads(pad, rows)
        for i in range(rows):
            north, above = north_of(i), above_of(i)
            south = beside(north[0:NZ], north[NZ:T2], 1, lane == 0)
            zero = jnp.zeros((1, 8, 128), F32)
            below = [
                jnp.concatenate([zero, above[t * NZ : t * NZ + NZ - 1]], axis=0) for t in (0, 1)
            ]
            storage, shade = storage_of(i), colour_of(i)
            for t in (0, 1):
                part = slice(t * NZ, t * NZ + NZ)
                west, east = pad[i + 1, part], pad[i + 2, part]
                six = (west, east, south[t], north[part], below[t], above[part])
                centre = storage[part] + west + east + south[t] + north[part] + below[t] + above[part]
                inverse = 1.0 / centre
                for k in range(6):
                    cfs[l][i, k, part] = six[k] * inverse
                ccs[l][i, part] = centre
                cis[l][i, part] = inverse
                cols[l][i, part] = shade[part]

    def pick0(k):
        return lambda i: f0[k, :, pl.ds(i, 8, stride=6), :]

    scaled(0, pick0(1), lambda i: raw[0, i], lambda i: raw[1, i], lambda i: raw[2, i], pick0(2))

    for m in range(3):
        even, odd = 2 * m, 2 * m + 1
        five = (
            f0[1, :, pl.ds(even, 8, stride=6), :] + f0[1, :, pl.ds(odd, 8, stride=6), :],
            raw[0, even],
            raw[1, even] + raw[1, odd],
            raw[2, even] + raw[2, odd],
            f0[2, :, pl.ds(even, 8, stride=6), :],
        )
        for k in range(5):
            ks[1][k * T2 : k * T2 + T2, pl.ds(4 + m, 8, stride=3), :] = five[k]
    for l in (2, 3):
        for k in range(5):
            part = slice(k * T2, k * T2 + T2)
            value = ks[l - 1][part, pl.ds(8, 8, stride=2), :]
            if k not in (1, 4):
                value = value + ks[l - 1][part, pl.ds(9, 8, stride=2), :]
            ks[l][part, 8:16] = value

    s_kn = [sems(len(NEAR[l])) for l in range(4)]
    s_kf = [sems(len(FAR[l])) for l in range(4)]
    s_rn = [sems(len(NEAR[l])) for l in range(4)]
    s_rf = [sems(len(FAR[l])) for l in range(4)]
    s_e = [sems(len(ITERATE[l])) for l in range(4)]
    s_ar = sems(22)

    def near_copies(l, src, own_at, dst, base, table):
        return [
            copy(src.at[:, own_at + a : own_at + b], dst.at[:, c:d], base + k, ring(right, 0))
            for k, (right, a, b, c, d) in enumerate(table)
        ]

    def far_copies(l, src, dst, base):
        return [
            copy(
                src.at[:, SO + a : SO + b], dst.at[k, :, c % 8 : c % 8 + 4], base + k, ring(right, 0)
            )
            for k, (right, a, b, c, d) in enumerate(FAR[l])
        ]

    def merge_far(l, far, dst):
        for k, (right, a, b, c, d) in enumerate(FAR[l]):
            dst[:, c:d] = far[k, :, c % 8 : c % 8 + 4]

    def keep_own(l, src, src_at, dst):
        n = OWN[l]
        dst[:, LO[l] : LO[l] + n] = src[:, src_at : src_at + n]
        if l == 3:
            dst[:, 28:32] = src[:, src_at : src_at + n]

    def kn_copies(l):
        return near_copies(l, ks[l], SO, kw[l], s_kn[l], NEAR[l])

    def kf_copies(l):
        return far_copies(l, ks[l], kf[l], s_kf[l])

    def rf_copies(l):
        return far_copies(l, sts[l], lrf[l], s_rf[l])

    def level_coefficients(l):
        def pick(k):
            return lambda i: kw[l][
                k * T2 : k * T2 + T2, pl.ds(WS[l] + i, 8, stride=ROWS[l]), :
            ]

        scaled(l, pick(0), pick(1), pick(2), pick(3), pick(4))

    def half(l, src, dst, shade):
        for i in range(ROWS[l]):
            for first in range(0, NZ, ZC):
                span, own, sums = neighbour_sum(cfs[l], src, i, first, first + ZC)
                for t in (0, 1):
                    fresh = rps[l][i, span[t]] + sums[t]
                    dst[i + 1, span[t]] = jnp.where(cols[l][i, span[t]] == shade, fresh, own[t])
        pads(dst, ROWS[l])

    def left_over(l, src, i, first, last):
        span, own, sums = neighbour_sum(cfs[l], src, i, first, last)
        return span, [
            ccs[l][i, span[t]] * (rps[l][i, span[t]] + sums[t] - own[t]) for t in (0, 1)
        ]

    def before(l, lin):
        ea, eb = eas[l], ebs[l]
        for i in range(ROWS[l]):
            scaled_rhs = lin[:, pl.ds(WS[l] + i, 8, stride=ROWS[l]), :] * cis[l][i]
            rps[l][i] = scaled_rhs
            ea[i + 1] = jnp.where(cols[l][i] == 0.0, scaled_rhs, 0.0)
        pads(ea, ROWS[l])
        half(l, ea, eb, 1.0)

        def sweep(j, carry):
            on = j < sweeps[l]
            half(l, eb, ea, jnp.where(on, 0.0, -1.0))
            half(l, ea, eb, jnp.where(on, 1.0, -1.0))
            return carry

        lax.fori_loop(1, 3, sweep, 0)

    def after(l):
        ea, eb = eas[l], ebs[l]

        def sweep(j, carry):
            on = j < sweeps[l]
            half(l, ea, eb, jnp.where(on, 0.0, -1.0))
            half(l, eb, ea, jnp.where(on, 1.0, -1.0))
            return carry

        lax.fori_loop(0, 3, sweep, 0)

    def restrict(l):
        stage, rows = sts[l + 1], ROWS[l] // 2

        for m in range(rows):
            for first in range(0, NZ, ZC):
                total = None
                for i in (2 * m, 2 * m + 1):
                    span, res = left_over(l, ebs[l], i, first, first + ZC)
                    if l == 0:
                        res = [rw[i, span[t]] * res[t] for t in (0, 1)]
                    total = res if total is None else [total[t] + res[t] for t in (0, 1)]
                for t in (0, 1):
                    stage[span[t], pl.ds(ST_OFF[l + 1] + m, 8, stride=rows), :] = total[t]

    def stage_iterate(l):
        for i in range(ROWS[l]):
            ess[l][:, pl.ds(ES_OFF[l] + i, 8, stride=ROWS[l]), :] = ebs[l][i + 1]

    def rn_copies(l):
        return near_copies(l, sts[l], SO, lrs[l], s_rn[l], NEAR[l])

    def e_copies(l):
        return near_copies(l, ess[l], ES_OFF[l] + HALO[l], els[l], s_e[l], ITERATE[l])

    def aggregate_ratio(cyc):
        s_a = s_ar + cyc * 11
        for first in range(0, NZ, ZC):
            for i in range(4):
                span, res = left_over(3, ebs[3], i, first, first + ZC)
                wlin[span[0], pl.ds(i, 8, stride=4), :] = res[0]
        for i in range(4):
            wlin[NZ:T2, pl.ds(i, 8, stride=4), :] = ccs[3][i, 0:NZ]
        total = jnp.zeros((3 * ARR, NAGG), F32)
        for i in range(4):
            for z in range(T2):
                agg[z : z + 1] = wlin[z, 12 + i : 13 + i, :]
            value = agg[...]
            high = value.astype(jnp.bfloat16)
            rest = value - high.astype(F32)
            middle = rest.astype(jnp.bfloat16)
            low = (rest - middle.astype(F32)).astype(jnp.bfloat16)
            three = jnp.concatenate([high.astype(F32), middle.astype(F32), low.astype(F32)], axis=0)
            total += lax.dot_general(
                three.astype(jnp.bfloat16), onehot[i], (((1,), (1,)), ((), ())),
                preferred_element_type=F32,
            )
        mine = total[0:ARR] + total[ARR : 2 * ARR] + total[2 * ARR :]
        low_half, high_half = mine[:, 0:256], mine[:, 256:512]
        ar_keep[...] = jnp.where(core == 0, low_half, high_half)
        ar_give[...] = jnp.where(core == 0, high_half, low_half)
        first_copy = copy(ar_give, ar_core.at[cyc], s_a, flip(0, 1))
        first_copy.start()
        stage_iterate(3)
        first_copy.wait()
        ar_sum[0] = ar_keep[...] + ar_core[cyc]
        at = 1
        for stage, group in enumerate((X_PARTNERS, Y_PARTNERS, Z_PARTNERS)):
            copies = [
                copy(ar_sum.at[stage], ar_in.at[cyc, stage, k], s_a + at + k, flip(*p))
                for k, p in enumerate(group)
            ]
            start(copies)
            if stage == 0:
                start(e_copies(3))
                keep_own(3, ess[3], 16, els[3])
            finish(copies)
            ar_sum[stage + 1] = ar_sum[stage] + ar_in[cyc, stage, 0] + ar_in[cyc, stage, 1] + ar_in[cyc, stage, 2]
            at += 3
        last_copy = copy(ar_sum.at[3], ar_last.at[cyc], s_a + 10, flip(0, 1))
        last_copy.start()
        last_copy.wait()
        mine, other = ar_sum[3], ar_last[cyc]
        low_half = jnp.where(core == 0, mine, other)
        high_half = jnp.where(core == 0, other, mine)
        ratio[0:NZ, 0:256] = low_half[0:NZ] / low_half[NZ:T2]
        ratio[0:NZ, 256:512] = high_half[0:NZ] / high_half[NZ:T2]

    def window_iterate(l, first):
        if l > 0:

            @pl.when(first)
            def _():
                finish(kf_copies(l))
                merge_far(l, kf[l], kw[l])
                level_coefficients(l)

            finish(rf_copies(l))
            merge_far(l, lrf[l], lrs[l])
            for i in range(ROWS[l]):
                rps[l][i] = lrs[l][:, pl.ds(WS[l] + i, 8, stride=ROWS[l]), :] * cis[l][i]
        finish(e_copies(l))
        for i in range(ROWS[l]):
            now = els[l][:, pl.ds(WS[l] + i, 8, stride=ROWS[l]), :]
            if l < 3:
                at = HALO[l + 1] - HALO[l] // 2 + i // 2
                now = now + cls[l + 1][:, pl.ds(at, 8, stride=ROWS[l] // 2), :]
            eas[l][i + 1] = now

    def add_aggregates():
        def row(i, carry):
            for t in (0, 1):
                where = idx[i, t]
                place, block = jnp.bitwise_and(where, 127), jnp.right_shift(where, 7)
                for z in range(NZ):
                    value = jnp.zeros((8, 128), F32)
                    for k in range(4):
                        table = jnp.broadcast_to(
                            ratio[z : z + 1, 128 * k : 128 * k + 128], (8, 128)
                        )
                        found = jnp.take_along_axis(table, place, axis=1)
                        value = jnp.where(block == k, found, value)
                    eas[3][i + 1, t * NZ + z] += value
            return carry

        lax.fori_loop(0, 4, row, 0)

    for l in (1, 2, 3):
        start(kn_copies(l))

    def cycle(cyc, carry):
        first = cyc == 0
        for l in range(4):
            before(l, f0.at[3] if l == 0 else lrs[l])
            if l < 3:
                restrict(l)
                start(rn_copies(l + 1))
                stage_iterate(l)
                if l > 0:
                    start(rf_copies(l))
                start(e_copies(l))
                if l == 2:
                    start(rf_copies(3))
                keep_own(l, ess[l], ES_OFF[l] + HALO[l], els[l])
                keep_own(l + 1, sts[l + 1], SO, lrs[l + 1])

                @pl.when(first)
                def _():
                    if l == 2:
                        for k in (3, 2, 1):
                            start(kf_copies(k))
                    keep_own(l + 1, ks[l + 1], SO, kw[l + 1])
                    finish(kn_copies(l + 1))
                    level_coefficients(l + 1)

                finish(rn_copies(l + 1))
        aggregate_ratio(cyc)
        for l in (3, 2, 1, 0):
            window_iterate(l, first)
            if l == 3:

                @pl.when(first)
                def _():
                    for i in range(4):
                        for t in (0, 1):
                            found = kw[3][100 + t, pl.ds(i, 8, stride=4), :]
                            idx[i, t] = found.astype(jnp.int32)

                add_aggregates()
            pads(eas[l], ROWS[l])
            after(l)
            if l > 0:
                for i in range(ROWS[l]):
                    cls[l][:, pl.ds(i, 8, stride=ROWS[l]), :] = eas[l][i + 1]

        for i in range(6):
            wlin[0:NZ, pl.ds(i, 8, stride=6), :] = eas[0][i + 1, 0:NZ]
        added = wlin[0:NZ, 8:40]

        @pl.when(first)
        def _():
            sol[...] = added

        @pl.when(jnp.logical_not(first))
        def _():
            sol[...] += added

        for i in range(6):
            for z in range(0, NZ, ZC):
                span, res = left_over(0, eas[0], i, z, z + ZC)
                wlin[span[0], pl.ds(i, 8, stride=6), :] = res[0]
        leftover = wlin[0:NZ, 8:40]

        @pl.when(first)
        def _():
            part = slice(3 * NZ, 4 * NZ)
            y0[part] = leftover
            pack(3)

            def fill_own():
                f0[3, 0:NZ, 8:40] = y0[part]

            y_exchange(part, fill_own)
            upper, lower = join(3)
            f0[3, NZ:T2, 8:24] = upper
            f0[3, NZ:T2, 24:40] = lower
            start(x_copies(slice(3, 4), f0, s_x))
            finish(x_copies(slice(3, 4), f0, s_x))

        @pl.when(jnp.logical_not(first))
        def _():
            fres[...] = leftover

        return carry

    lax.fori_loop(0, 2, cycle, 0)


def on_device(gxn, gyn, perm, stor, act, colour, rweight, sweeps, amap, source):
    def vm(*shape, dtype=F32):
        return pltpu.VMEM(shape, dtype)

    levels = range(LEVELS)
    scratch = [
        vm(50, 32, 128),
        vm(2, 51, 16, 128),
        vm(2, 51, 16, 128),
        vm(4, T2, 48, 128),
        vm(6, T2, 8, 128),
        vm(3, 6, T2, 8, 128),
        [vm(ROWS[l], 6, T2, 8, 128) for l in levels],
        [vm(ROWS[l], T2, 8, 128) for l in levels],
        [vm(ROWS[l], T2, 8, 128) for l in levels],
        [vm(ROWS[l], T2, 8, 128) for l in levels],
        [vm(ROWS[l], T2, 8, 128) for l in levels],
        [vm(ROWS[l] + 2, T2, 8, 128) for l in levels],
        [vm(ROWS[l] + 2, T2, 8, 128) for l in levels],
        [vm(102 if l == 3 else 100, ST_ROWS[l], 128) for l in levels],
        [vm(102 if l == 3 else 100, LIN[l], 128) for l in levels],
        [vm(2, 102 if l == 3 else 100, 8, 128) for l in levels],
        [vm(T2, ST_ROWS[l], 128) for l in levels],
        [vm(T2, LIN[l], 128) for l in levels],
        [vm(2, T2, 8, 128) for l in levels],
        [vm(T2, ES_ROWS[l], 128) for l in levels],
        [vm(T2, LIN[l], 128) for l in levels],
        [vm(T2, 8 * ROWS[l], 128) for l in levels],
        vm(4, 2, 8, 128, dtype=jnp.int32),
        vm(4, NAGG, 128, dtype=jnp.bfloat16),
        vm(ARR, 128),
        vm(ARR, 256),
        vm(ARR, 256),
        vm(2, ARR, 256),
        vm(4, ARR, 256),
        vm(2, 3, 3, ARR, 256),
        vm(2, ARR, 256),
        vm(16, NAGG),
        vm(T2, 48, 128),
        pltpu.SemaphoreType.DMA((80,)),
        pltpu.SemaphoreType.DMA((80,)),
    ]
    vmem = pl.BlockSpec(memory_space=pltpu.VMEM)
    smem = pl.BlockSpec(memory_space=pltpu.SMEM)
    out = jax.ShapeDtypeStruct(perm.shape, F32)
    return pl.pallas_call(
        functools.partial(kernel, gxn, gyn),
        out_shape=(out, out),
        in_specs=[vmem, vmem, vmem, vmem, vmem, smem, vmem, vmem],
        out_specs=(vmem, vmem),
        scratch_shapes=scratch,
        compiler_params=pltpu.CompilerParams(
            collective_id=0, has_side_effects=True, vmem_limit_bytes=60 * 2**20
        ),
    )(perm, stor, act, colour, rweight, sweeps, amap, source)


def solution(mesh):
    field = P(None, "gx", "gy")
    column = P("gx", "gy")
    return jax.shard_map(
        functools.partial(on_device, mesh.shape["gx"], mesh.shape["gy"]),
        mesh=mesh,
        in_specs=(field, field, column, field, field, P(), column, field),
        out_specs=(field, field),
        check_vma=False,
    )
```

```python
import functools
import jax
import jax.numpy as jnp
from jax import lax
from jax.experimental import pallas as pl
from jax.experimental.pallas import tpu as pltpu
from jax.sharding import PartitionSpec as P

MESH = pl.DeviceIdType.MESH
F32 = jnp.float32
NZ = 10
T2 = 2 * NZ
LEVELS = 4
NAGG = 512
ROWS = (6, 6, 4, 4)
HALO = (8, 16, 12, 12)
OWN = (32, 16, 8, 4)
LIN = (48, 48, 40, 32)
LO = (8, 16, 16, 12)
WS = (8, 0, 4, 0)
NEAR = (
    (),
    ((1, 8, 16, 8, 16), (-1, 0, 8, 32, 40)),
    ((1, 0, 8, 8, 16), (-1, 0, 8, 24, 32)),
    ((1, 0, 4, 8, 12), (-1, 0, 4, 16, 20), (2, 0, 4, 4, 8), (-2, 0, 4, 20, 24)),
)
FAR = (
    (),
    ((1, 4, 8, 4, 8), (-1, 8, 12, 40, 44)),
    ((2, 4, 8, 4, 8), (-2, 0, 4, 32, 36)),
    ((3, 0, 4, 0, 4), (-3, 0, 4, 24, 28)),
)
ITERATE = (
    ((1, 24, 32, 0, 8), (-1, 0, 8, 40, 48)),
    ((1, 4, 16, 4, 16), (-1, 0, 12, 32, 44)),
    NEAR[2] + FAR[2],
    NEAR[3] + FAR[3],
)
SO = 8
ST_ROWS = (48, 32, 24, 24)
ST_OFF = (0, 4, 0, 2)
ES_OFF = (0, 0, 4, 4)
ES_ROWS = (48, 48, 40, 40)
ARR = 24
ZC = 2

X_PARTNERS = ((1, 0), (2, 0), (3, 0), (0, 1), (1, 1), (2, 1), (3, 1))
Y_PARTNERS = ((8, 0), (16, 0), (24, 0))
Z_PARTNERS = ((4, 0), (0, 2), (4, 2), (0, 1), (4, 1), (0, 3), (4, 3))


def pads(buf, rows):
    buf[0] = pltpu.roll(buf[rows], 1, 1)
    buf[rows + 1] = pltpu.roll(buf[1], 7, 1)


def beside(own, other, shift, edge):
    moved, moved_other = pltpu.roll(own, shift, 2), pltpu.roll(other, shift, 2)
    return jnp.where(edge, moved_other, moved), jnp.where(edge, moved, moved_other)


def zshift(buf, row, values, tile, first, last, up):
    base = tile * NZ
    if up:
        tail = values[-1:] if last == NZ else buf[row, base + last : base + last + 1]
        return jnp.concatenate([values[1:], tail], axis=0) if last - first > 1 else tail
    head = values[:1] if first == 0 else buf[row, base + first - 1 : base + first]
    return jnp.concatenate([head, values[:-1]], axis=0) if last - first > 1 else head


def neighbour_sum(cf, src, i, first, last):
    lane = lax.broadcasted_iota(jnp.int32, (last - first, 8, 128), 2)
    span = [slice(t * NZ + first, t * NZ + last) for t in (0, 1)]
    own = [src[i + 1, span[t]] for t in (0, 1)]
    south = beside(own[0], own[1], 1, lane == 0)
    north = beside(own[0], own[1], 127, lane == 127)
    sums = []
    for t in (0, 1):
        acc = cf[i, 0, span[t]] * src[i, span[t]]
        acc += cf[i, 1, span[t]] * src[i + 2, span[t]]
        acc += cf[i, 4, span[t]] * zshift(src, i + 1, own[t], t, first, last, False)
        acc += cf[i, 5, span[t]] * zshift(src, i + 1, own[t], t, first, last, True)
        acc += cf[i, 2, span[t]] * south[t]
        acc += cf[i, 3, span[t]] * north[t]
        sums.append(acc)
    return span, own, sums


def kernel(
    gxn,
    gyn,
    perm,
    stor,
    act,
    colour,
    rweight,
    sweeps,
    amap,
    source,
    sol,
    fres,
    yp,
    pw,
    fc,
    fh,
    rw,
    raw,
    p8,
    cfs,
    ccs,
    cis,
    cols,
    rps,
    eas,
    ebs,
    ks,
    kw,
    kf,
    kfw,
    sts,
    lrs,
    lrf,
    ess,
    els,
    cls,
    idx,
    onehot,
    agg,
    ar_keep,
    ar_give,
    ar_sum,
    ar_in,
    ratio,
    wlin,
    send,
    recv,
):
    gx, gy = lax.axis_index("gx"), lax.axis_index("gy")
    core = lax.rem(gy, 2)

    def ring(dx, dy):
        return (lax.rem(gx + dx + gxn, gxn), lax.rem(gy + dy + gyn, gyn))

    def flip(dx, dy):
        return (jnp.bitwise_xor(gx, dx), jnp.bitwise_xor(gy, dy))

    counter = [0]

    def sems(n):
        counter[0] += n
        return counter[0] - n

    def copy(src, dst, sem, device):
        return pltpu.make_async_remote_copy(
            src_ref=src, dst_ref=dst, send_sem=send.at[sem], recv_sem=recv.at[sem],
            device_id=device, device_id_type=MESH,
        )

    def start(copies):
        for c in copies:
            c.start()

    def finish(copies):
        for c in copies:
            c.wait()

    barrier = pltpu.get_barrier_semaphore()
    partners = [ring(d, 0) for d in (1, -1, 2, -2, 3, -3)] + [ring(dx, dy) for dx in (-1, 0, 1) for dy in (-1, 1)]
    partners += [flip(*p) for p in X_PARTNERS + Y_PARTNERS + Z_PARTNERS]
    for device in partners:
        pl.semaphore_signal(barrier, inc=1, device_id=device, device_id_type=MESH)

    lane = lax.broadcasted_iota(jnp.int32, (NZ, 8, 128), 2)
    sub = lax.broadcasted_iota(jnp.int32, (NZ, 8, 128), 1)
    layer = lax.broadcasted_iota(jnp.int32, (NZ, 8, 128), 0)

    def pack(k, value):
        part = slice(k * NZ, k * NZ + NZ)
        for h in (0, 1):
            v0, v1 = value[:, 16 * h : 16 * h + 8], value[:, 16 * h + 8 : 16 * h + 16]
            a = jnp.where(sub < 4, v0, pltpu.roll(v1, 4, 1))
            b = jnp.where(sub < 4, pltpu.roll(v0, 4, 1), v1)
            rows = slice(8 * h, 8 * h + 8)
            yp[0, part, rows] = jnp.where(lane < 64, pltpu.roll(a, 64, 2), b)
            yp[1, part, rows] = jnp.where(lane < 64, a, pltpu.roll(b, 64, 2))

    def unpack(k, h, dst, at, to):
        part = slice(k * NZ, k * NZ + NZ)
        left, right = pw[0, part, 8 * h : 8 * h + 8], pw[1, part, 8 * h : 8 * h + 8]
        a = jnp.where(lane < 64, right, pltpu.roll(left, 64, 2))
        b = jnp.where(lane < 64, pltpu.roll(right, 64, 2), left)
        dst[to, at : at + 8] = jnp.where(sub < 4, a, pltpu.roll(b, 4, 1))
        dst[to, at + 8 : at + 16] = jnp.where(sub < 4, pltpu.roll(a, 4, 1), b)

    active = act[...] > 0
    for z in range(NZ):
        fc[z, 16:48] = jnp.where(active, perm[z], 0.0)
        fc[NZ + z, 16:48] = jnp.where(active, stor[z], 1.0)
        fc[2 * NZ + z, 16:48] = colour[z].astype(F32)
        fc[3 * NZ + z, 16:48] = source[z]
    for k in range(4):
        pack(k, fc[k * NZ : k * NZ + NZ, 16:48])
    pack(4, rweight[...])
    own_map = amap[...].astype(F32)
    yp[0, 50, 0:4] = own_map
    yp[1, 50, 0:4] = own_map

    RAW, RHS = slice(0, 30), slice(30, 40)
    s_y, s_xr, s_xs, s_cr, s_cs = sems(2), sems(2), sems(2), sems(4), sems(4)

    def beside_copies(v, span, raw_too):
        dy = 1 - 2 * v
        out = [copy(yp.at[v, span], pw.at[v, span, 8:24], s_y + v, ring(0, dy))]
        for q, (dx, a, to) in enumerate(((1, 12, 4), (-1, 0, 24))):
            out.append(
                copy(
                    yp.at[v, RHS, a : a + 4], pw.at[v, RHS, to : to + 4],
                    s_cs + 2 * v + q, ring(dx, dy),
                )
            )
        if raw_too:
            for q, (dx, a, to) in enumerate(((1, 8, 0), (-1, 0, 24))):
                out.append(
                    copy(
                        yp.at[v, RAW, a : a + 8], pw.at[v, RAW, to : to + 8],
                        s_cr + 2 * v + q, ring(dx, dy),
                    )
                )
        return out

    def exchange(span, raw_too, between):
        along = [
            copy(fc.at[RHS, 40:48], fc.at[RHS, 8:16], s_xs, ring(1, 0)),
            copy(fc.at[RHS, 16:24], fc.at[RHS, 48:56], s_xs + 1, ring(-1, 0)),
        ]
        if raw_too:
            along = [
                copy(fc.at[RAW, 32:48], fc.at[RAW, 0:16], s_xr, ring(1, 0)),
                copy(fc.at[RAW, 16:32], fc.at[RAW, 48:64], s_xr + 1, ring(-1, 0)),
            ] + along
        up, down = beside_copies(0, span, raw_too), beside_copies(1, span, raw_too)
        start(along)

        @pl.when(gy < gyn - 1)
        def _():
            start(up)

        @pl.when(gy > 0)
        def _():
            start(down)

        for v, edge in ((0, gy == 0), (1, gy == gyn - 1)):

            @pl.when(edge)
            def _():
                pw[v, span, 8:24] = yp[v, span]
                parts = (RAW, RHS) if raw_too else (RHS,)
                for part in parts:
                    pw[v, part, 0:8] = yp[v, part, 8:16]
                    pw[v, part, 24:32] = yp[v, part, 0:8]

        between()
        finish(along)

        @pl.when(gy < gyn - 1)
        def _():
            for c in up:
                c.wait_send()
            for c in down:
                c.wait_recv()

        @pl.when(gy > 0)
        def _():
            for c in down:
                c.wait_send()
            for c in up:
                c.wait_recv()

    def fill():
        for j in range(4):
            agg_id = lax.broadcasted_iota(jnp.int32, (NAGG, 128), 0)
            onehot[j] = (agg_id == amap[j : j + 1, :]).astype(jnp.bfloat16)
        agg[...] = jnp.zeros_like(agg)
        wlin[...] = jnp.zeros_like(wlin)
        for at, end in ((0, 8), (40, 48)):
            kw[1][:, at:end] = jnp.ones((100, end - at, 128), F32)
        for l in (2, 3):
            for _, _, _, at, end in FAR[l]:
                kw[l][0:100, at:end] = jnp.ones((100, end - at, 128), F32)
        for _, _, _, at, end in FAR[3]:
            kw[3][100:102, at:end] = jnp.zeros((2, end - at, 128), F32)
        wlin[0:NZ, 8:40] = rweight[...]
        for i in range(6):
            rw[i, 0:NZ] = wlin[0:NZ, pl.ds(i, 8, stride=6), :]

    for l in (1, 2, 3):
        lrs[l][...] = jnp.zeros_like(lrs[l])
        els[l][...] = jnp.zeros_like(els[l])
    pl.semaphore_wait(barrier, len(partners))
    exchange(slice(0, 51), True, fill)
    for k in range(4):
        for h in range(4):
            unpack(k, h, fh, 16 * h, slice(k * NZ, k * NZ + NZ))
    for h in (1, 2):
        unpack(4, h, wlin, 16 * h - 8, slice(NZ, T2))
    for i in range(6):
        rw[i, NZ:T2] = wlin[NZ:T2, pl.ds(i, 8, stride=6), :]
    mlane = lax.broadcasted_iota(jnp.int32, (4, 128), 1)
    ks[3][100, 8:12] = own_map
    ks[3][101, 8:12] = jnp.where(mlane < 64, pw[1, 50, 8:12], pw[0, 50, 8:12])

    def raw_rows(k, at, stride):
        part = slice(k * NZ, k * NZ + NZ)
        rows = pl.ds(at, 8, stride=stride)
        return jnp.concatenate([fc[part, rows, :], fh[part, rows, :]], axis=0)

    for i in range(8):
        p8[i + 1] = raw_rows(0, i, 8)
    pads(p8, 8)

    def harmonic(a, b):
        total = a + b
        return jnp.where(total > 0, 2.0 * a * b / jnp.where(total > 0, total, 1.0), 0.0)

    for m in range(4):
        pair = []
        for i in (2 * m, 2 * m + 1):
            own = [p8[i + 1, t * NZ : t * NZ + NZ] for t in (0, 1)]
            north = beside(own[0], own[1], 127, lane == 127)
            xg = gx * 32 - 16 + 8 * sub + i
            three = [[], [], []]
            for t in (0, 1):
                part = slice(t * NZ, t * NZ + NZ)
                yg = gy * 128 + lane
                if t == 1:
                    yg = jnp.where(lane < 64, yg + 128, yg - 128)
                west = harmonic(own[t], p8[i, part])
                above = 0.5 * harmonic(own[t], zshift(p8, i + 1, own[t], t, 0, NZ, True))
                three[0].append(jnp.where((xg == 0) | (xg == 1024), 0.0, west))
                three[1].append(
                    jnp.where(jnp.bitwise_and(yg, 511) == 511, 0.0, harmonic(own[t], north[t]))
                )
                three[2].append(jnp.where(layer == NZ - 1, 0.0, above))
            three = [jnp.concatenate(f, axis=0) for f in three]
            for k in range(3):
                raw[k, :, pl.ds(i, 8, stride=8), :] = three[k]
            pair.append(three)
        five = (
            raw_rows(1, 2 * m, 8) + raw_rows(1, 2 * m + 1, 8),
            pair[0][0],
            pair[0][1] + pair[1][1],
            pair[0][2] + pair[1][2],
            raw_rows(2, 2 * m, 8),
        )
        for k in range(5):
            kw[1][k * T2 : k * T2 + T2, pl.ds(8 + m, 8, stride=4), :] = five[k]

    for l, finer, at in ((2, kw[1], 16), (3, ks[2], 8)):
        for k in range(5):
            part = slice(k * T2, k * T2 + T2)
            value = finer[part, pl.ds(at, 8, stride=2), :]
            if k not in (1, 4):
                value = value + finer[part, pl.ds(at + 1, 8, stride=2), :]
            ks[l][part, 8:16] = value

    def scaled(l, storage_of, west_of, north_of, above_of, colour_of):
        rows, pad = ROWS[l], eas[l]
        for i in range(rows):
            pad[i + 1] = west_of(i)
        pads(pad, rows)
        for i in range(rows):
            north, above = north_of(i), above_of(i)
            south = beside(north[0:NZ], north[NZ:T2], 1, lane == 0)
            zero = jnp.zeros((1, 8, 128), F32)
            below = [
                jnp.concatenate([zero, above[t * NZ : t * NZ + NZ - 1]], axis=0) for t in (0, 1)
            ]
            storage, shade = storage_of(i), colour_of(i)
            for t in (0, 1):
                part = slice(t * NZ, t * NZ + NZ)
                west, east = pad[i + 1, part], pad[i + 2, part]
                six = (west, east, south[t], north[part], below[t], above[part])
                centre = storage[part] + west + east + south[t] + north[part] + below[t] + above[part]
                inverse = 1.0 / centre
                for k in range(6):
                    cfs[l][i, k, part] = six[k] * inverse
                ccs[l][i, part] = centre
                cis[l][i, part] = inverse
                cols[l][i, part] = shade[part]

    def face0(k):
        return lambda i: raw[k, :, pl.ds(WS[0] + i, 8, stride=6), :]

    def raw0(k):
        return lambda i: raw_rows(k, WS[0] + i, 6)

    s_kn = [sems(len(NEAR[l])) for l in range(4)]
    s_kf = [sems(len(FAR[l])) for l in range(4)]
    s_rn = [sems(len(NEAR[l])) for l in range(4)]
    s_rf = [sems(len(FAR[l])) for l in range(4)]
    s_e = [sems(len(ITERATE[l])) for l in range(4)]
    s_ar = sems(34)
    s_kw = sems(1)

    def near_copies(l, src, own_at, dst, base, table):
        return [
            copy(src.at[:, own_at + a : own_at + b], dst.at[:, c:d], base + k, ring(right, 0))
            for k, (right, a, b, c, d) in enumerate(table)
        ]

    def far_copies(l, src, own_at, dst, base):
        return [
            copy(
                src.at[:, own_at + a : own_at + b], dst.at[k, :, c % 8 : c % 8 + 4], base + k, ring(right, 0)
            )
            for k, (right, a, b, c, d) in enumerate(FAR[l])
        ]

    def merge_far(l, far, dst):
        for k, (right, a, b, c, d) in enumerate(FAR[l]):
            dst[:, c:d] = far[k, :, c % 8 : c % 8 + 4]

    def keep_own(l, src, src_at, dst):
        n = OWN[l]
        dst[:, LO[l] : LO[l] + n] = src[:, src_at : src_at + n]
        if l == 3:
            dst[:, 28:32] = src[:, src_at : src_at + n]

    def kn_copies(l):
        return near_copies(l, ks[l], SO, kw[l], s_kn[l], NEAR[l])

    def kf_copies(l):
        if l > 1:
            return far_copies(l, ks[l], SO, kf[l], s_kf[l])
        west = slice(T2, 2 * T2)
        return far_copies(1, kw[1], LO[1], kf[1], s_kf[1]) + [
            copy(kw[1].at[west, 24:28], kfw.at[:, 0:4], s_kw, ring(1, 0))
        ]

    def rf_copies(l):
        return far_copies(l, sts[l], SO, lrf[l], s_rf[l])

    def level_coefficients(l):
        def pick(k):
            return lambda i: kw[l][
                k * T2 : k * T2 + T2, pl.ds(WS[l] + i, 8, stride=ROWS[l]), :
            ]

        scaled(l, pick(0), pick(1), pick(2), pick(3), pick(4))

    def half(l, src, dst, shade):
        for i in range(ROWS[l]):
            for first in range(0, NZ, ZC):
                span, own, sums = neighbour_sum(cfs[l], src, i, first, first + ZC)
                for t in (0, 1):
                    fresh = rps[l][i, span[t]] + sums[t]
                    dst[i + 1, span[t]] = jnp.where(cols[l][i, span[t]] == shade, fresh, own[t])
        pads(dst, ROWS[l])

    def left_over(l, src, i, first, last):
        span, own, sums = neighbour_sum(cfs[l], src, i, first, last)
        return span, [
            ccs[l][i, span[t]] * (rps[l][i, span[t]] + sums[t] - own[t]) for t in (0, 1)
        ]

    def before(l):
        ea, eb = eas[l], ebs[l]
        for i in range(ROWS[l]):
            if l == 0:
                scaled_rhs = raw_rows(3, WS[0] + i, 6) * cis[0][i]
            else:
                scaled_rhs = lrs[l][:, pl.ds(WS[l] + i, 8, stride=ROWS[l]), :] * cis[l][i]
            rps[l][i] = scaled_rhs
            ea[i + 1] = jnp.where(cols[l][i] == 0.0, scaled_rhs, 0.0)
        pads(ea, ROWS[l])
        half(l, ea, eb, 1.0)

        def sweep(j, carry):
            on = j < sweeps[l]
            half(l, eb, ea, jnp.where(on, 0.0, -1.0))
            half(l, ea, eb, jnp.where(on, 1.0, -1.0))
            return carry

        lax.fori_loop(1, 3, sweep, 0)

    def after(l):
        ea, eb = eas[l], ebs[l]

        def sweep(j, carry):
            on = j < sweeps[l]
            half(l, ea, eb, jnp.where(on, 0.0, -1.0))
            half(l, eb, ea, jnp.where(on, 1.0, -1.0))
            return carry

        lax.fori_loop(0, 3, sweep, 0)

    def restrict(l):
        stage, rows = sts[l + 1], ROWS[l] // 2

        for m in range(rows):
            for first in range(0, NZ, ZC):
                total = None
                for i in (2 * m, 2 * m + 1):
                    span, res = left_over(l, ebs[l], i, first, first + ZC)
                    if l == 0:
                        res = [rw[i, span[t]] * res[t] for t in (0, 1)]
                    total = res if total is None else [total[t] + res[t] for t in (0, 1)]
                for t in (0, 1):
                    stage[span[t], pl.ds(ST_OFF[l + 1] + m, 8, stride=rows), :] = total[t]

    def stage_iterate(l):
        for i in range(ROWS[l]):
            ess[l][:, pl.ds(ES_OFF[l] + i, 8, stride=ROWS[l]), :] = ebs[l][i + 1]

    def rn_copies(l):
        return near_copies(l, sts[l], SO, lrs[l], s_rn[l], NEAR[l])

    def e_copies(l):
        return near_copies(l, ess[l], ES_OFF[l] + HALO[l], els[l], s_e[l], ITERATE[l])

    def aggregate_ratio(cyc):
        s_a = s_ar + cyc * 17
        for first in range(0, NZ, ZC):
            for i in range(4):
                span, res = left_over(3, ebs[3], i, first, first + ZC)
                wlin[span[0], pl.ds(i, 8, stride=4), :] = res[0]
        for i in range(4):
            wlin[NZ:T2, pl.ds(i, 8, stride=4), :] = ccs[3][i, 0:NZ]
        total = jnp.zeros((3 * ARR, NAGG), F32)
        for i in range(4):
            for z in range(T2):
                agg[z : z + 1] = wlin[z, 12 + i : 13 + i, :]
            value = agg[...]
            high = value.astype(jnp.bfloat16)
            rest = value - high.astype(F32)
            middle = rest.astype(jnp.bfloat16)
            low = (rest - middle.astype(F32)).astype(jnp.bfloat16)
            three = jnp.concatenate([high.astype(F32), middle.astype(F32), low.astype(F32)], axis=0)
            total += lax.dot_general(
                three.astype(jnp.bfloat16), onehot[i], (((1,), (1,)), ((), ())),
                preferred_element_type=F32,
            )
        mine = total[0:ARR] + total[ARR : 2 * ARR] + total[2 * ARR :]
        low_half, high_half = mine[:, 0:256], mine[:, 256:512]
        ar_keep[...] = jnp.where(core == 0, low_half, high_half)
        ar_give[...] = jnp.where(core == 0, high_half, low_half)
        stage_iterate(3)
        at = s_a
        for stage, group in enumerate((X_PARTNERS, Y_PARTNERS, Z_PARTNERS)):
            copies = []
            for k, p in enumerate(group):
                src = ar_sum.at[stage]
                if stage == 0:
                    src = ar_give if p[1] else ar_keep
                copies.append(copy(src, ar_in.at[cyc, stage, k], at + k, flip(*p)))
            at += len(group)
            start(copies)
            if stage == 0:
                start(e_copies(3) + e_copies(2) + rf_copies(2))

                @pl.when(cyc == 0)
                def _():
                    start(kf_copies(2))

                keep_own(3, ess[3], 16, els[3])
            if stage == 2:

                @pl.when(cyc == 0)
                def _():
                    start(kf_copies(1))

            finish(copies)
            mine = ar_keep[...] if stage == 0 else ar_sum[stage]
            for k in range(7 if stage == 0 else 3):
                mine = mine + ar_in[cyc, stage, k]
            if stage < 2:
                ar_sum[stage + 1] = mine
        other = ar_in[cyc, 2, 3] + ar_in[cyc, 2, 4] + ar_in[cyc, 2, 5] + ar_in[cyc, 2, 6]
        low_half = jnp.where(core == 0, mine, other)
        high_half = jnp.where(core == 0, other, mine)
        ratio[0:NZ, 0:256] = low_half[0:NZ] / low_half[NZ:T2]
        ratio[0:NZ, 256:512] = high_half[0:NZ] / high_half[NZ:T2]

    def window_iterate(l, first):
        if l > 0:

            @pl.when(first)
            def _():
                finish(kf_copies(l))
                merge_far(l, kf[l], kw[l])
                if l == 1:
                    kw[1][T2 : 2 * T2, 8:12] = kfw[:, 0:4]
                level_coefficients(l)

            finish(rf_copies(l))
            merge_far(l, lrf[l], lrs[l])
            for i in range(ROWS[l]):
                rps[l][i] = lrs[l][:, pl.ds(WS[l] + i, 8, stride=ROWS[l]), :] * cis[l][i]
        finish(e_copies(l))
        for i in range(ROWS[l]):
            at = 0 if l == 0 else WS[l]
            now = els[l][:, pl.ds(at + i, 8, stride=ROWS[l]), :]
            if l < 3:
                at = HALO[l + 1] - HALO[l] // 2 + i // 2
                now = now + cls[l + 1][:, pl.ds(at, 8, stride=ROWS[l] // 2), :]
            eas[l][i + 1] = now

    def add_aggregates():
        def row(i, carry):
            for t in (0, 1):
                where = idx[i, t]
                place, block = jnp.bitwise_and(where, 127), jnp.right_shift(where, 7)
                for z in range(NZ):
                    value = jnp.zeros((8, 128), F32)
                    for k in range(4):
                        table = jnp.broadcast_to(
                            ratio[z : z + 1, 128 * k : 128 * k + 128], (8, 128)
                        )
                        found = jnp.take_along_axis(table, place, axis=1)
                        value = jnp.where(block == k, found, value)
                    eas[3][i + 1, t * NZ + z] += value
            return carry

        lax.fori_loop(0, 4, row, 0)

    start(kn_copies(2))
    scaled(0, raw0(1), face0(0), face0(1), face0(2), raw0(2))

    def cycle(cyc, carry):
        first = cyc == 0
        for l in range(4):
            before(l)
            if l < 3:
                restrict(l)
                start(rn_copies(l + 1))

                @pl.when(first)
                def _():
                    start(kn_copies(3) if l == 0 else kf_copies(3) if l == 2 else [])

                stage_iterate(l)
                if l == 1:
                    start(rf_copies(1))
                start(e_copies(l) if l < 2 else rf_copies(3))
                keep_own(l, ess[l], ES_OFF[l] + HALO[l], els[l])
                keep_own(l + 1, sts[l + 1], SO, lrs[l + 1])

                @pl.when(first)
                def _():
                    if l > 0:
                        keep_own(l + 1, ks[l + 1], SO, kw[l + 1])
                        finish(kn_copies(l + 1))
                    level_coefficients(l + 1)

                finish(rn_copies(l + 1))
        aggregate_ratio(cyc)
        for l in (3, 2, 1, 0):
            window_iterate(l, first)
            if l == 3:

                @pl.when(first)
                def _():
                    for i in range(4):
                        for t in (0, 1):
                            found = kw[3][100 + t, pl.ds(i, 8, stride=4), :]
                            idx[i, t] = found.astype(jnp.int32)

                add_aggregates()
            pads(eas[l], ROWS[l])
            after(l)
            if l > 0:
                for i in range(ROWS[l]):
                    cls[l][:, pl.ds(i, 8, stride=ROWS[l]), :] = eas[l][i + 1]

        for i in range(6):
            for z in range(0, NZ, ZC):
                span, res = left_over(0, eas[0], i, z, z + ZC)
                wlin[span[0], pl.ds(i, 8, stride=6), :] = res[0]
        leftover = wlin[0:NZ, 8:40]

        def result():
            for i in range(6):
                wlin[0:NZ, pl.ds(i, 8, stride=6), :] = eas[0][i + 1, 0:NZ]
            return wlin[0:NZ, 8:40]

        @pl.when(first)
        def _():
            fc[RHS, 16:48] = leftover
            pack(3, leftover)

            def keep():
                sol[...] = result()

            exchange(RHS, False, keep)
            for h in range(4):
                unpack(3, h, fh, 16 * h, RHS)

        @pl.when(jnp.logical_not(first))
        def _():
            fres[...] = leftover
            sol[...] += result()

        return carry

    lax.fori_loop(0, 2, cycle, 0)


def on_device(gxn, gyn, perm, stor, act, colour, rweight, sweeps, amap, source):
    def vm(*shape, dtype=F32):
        return pltpu.VMEM(shape, dtype)

    levels = range(LEVELS)
    scratch = [
        vm(2, 51, 16, 128),
        vm(2, 51, 32, 128),
        vm(40, 64, 128),
        vm(40, 64, 128),
        vm(6, T2, 8, 128),
        vm(3, T2, 64, 128),
        vm(10, T2, 8, 128),
        [vm(ROWS[l], 6, T2, 8, 128) for l in levels],
        [vm(ROWS[l], T2, 8, 128) for l in levels],
        [vm(ROWS[l], T2, 8, 128) for l in levels],
        [vm(ROWS[l], T2, 8, 128) for l in levels],
        [vm(ROWS[l], T2, 8, 128) for l in levels],
        [vm(ROWS[l] + 2, T2, 8, 128) for l in levels],
        [vm(ROWS[l] + 2, T2, 8, 128) for l in levels],
        [vm(102 if l == 3 else 100, ST_ROWS[l], 128) for l in levels],
        [vm(102 if l == 3 else 100, LIN[l], 128) for l in levels],
        [vm(2, 102 if l == 3 else 100, 8, 128) for l in levels],
        vm(T2, 8, 128),
        [vm(T2, ST_ROWS[l], 128) for l in levels],
        [vm(T2, LIN[l], 128) for l in levels],
        [vm(2, T2, 8, 128) for l in levels],
        [vm(T2, ES_ROWS[l], 128) for l in levels],
        [vm(T2, LIN[l], 128) for l in levels],
        [vm(T2, 8 * ROWS[l], 128) for l in levels],
        vm(4, 2, 8, 128, dtype=jnp.int32),
        vm(4, NAGG, 128, dtype=jnp.bfloat16),
        vm(ARR, 128),
        vm(ARR, 256),
        vm(ARR, 256),
        vm(4, ARR, 256),
        vm(2, 3, 7, ARR, 256),
        vm(16, NAGG),
        vm(T2, 48, 128),
        pltpu.SemaphoreType.DMA((112,)),
        pltpu.SemaphoreType.DMA((112,)),
    ]
    vmem = pl.BlockSpec(memory_space=pltpu.VMEM)
    smem = pl.BlockSpec(memory_space=pltpu.SMEM)
    out = jax.ShapeDtypeStruct(perm.shape, F32)
    return pl.pallas_call(
        functools.partial(kernel, gxn, gyn),
        out_shape=(out, out),
        in_specs=[vmem, vmem, vmem, vmem, vmem, smem, vmem, vmem],
        out_specs=(vmem, vmem),
        scratch_shapes=scratch,
        compiler_params=pltpu.CompilerParams(
            collective_id=0, has_side_effects=True, vmem_limit_bytes=60 * 2**20
        ),
    )(perm, stor, act, colour, rweight, sweeps, amap, source)


def solution(mesh):
    field = P(None, "gx", "gy")
    column = P("gx", "gy")
    return jax.shard_map(
        functools.partial(on_device, mesh.shape["gx"], mesh.shape["gy"]),
        mesh=mesh,
        in_specs=(field, field, column, field, field, P(), column, field),
        out_specs=(field, field),
        check_vma=False,
    )
```

```python
import functools
import jax
import jax.numpy as jnp
from jax import lax
from jax.experimental import pallas as pl
from jax.experimental.pallas import tpu as pltpu
from jax.sharding import PartitionSpec as P

MESH = pl.DeviceIdType.MESH
F32 = jnp.float32
NZ = 10
T2 = 2 * NZ
LEVELS = 4
NAGG = 512
ROWS = (6, 6, 4, 4)
HALO = (8, 16, 12, 12)
OWN = (32, 16, 8, 4)
LIN = (48, 48, 40, 32)
LO = (8, 16, 16, 12)
WS = (8, 0, 4, 0)
NEAR = (
    (),
    ((1, 8, 16, 8, 16), (-1, 0, 8, 32, 40)),
    ((1, 0, 8, 8, 16), (-1, 0, 8, 24, 32)),
    ((1, 0, 4, 8, 12), (-1, 0, 4, 16, 20), (2, 0, 4, 4, 8), (-2, 0, 4, 20, 24)),
)
FAR = (
    (),
    ((1, 4, 8, 4, 8), (-1, 8, 12, 40, 44)),
    ((2, 4, 8, 4, 8), (-2, 0, 4, 32, 36)),
    ((3, 0, 4, 0, 4), (-3, 0, 4, 24, 28)),
)
ITERATE = (
    ((1, 24, 32, 0, 8), (-1, 0, 8, 40, 48)),
    ((1, 4, 16, 4, 16), (-1, 0, 12, 32, 44)),
    NEAR[2] + FAR[2],
    NEAR[3] + FAR[3],
)
SO = 8
ST_ROWS = (48, 32, 24, 24)
ST_OFF = (0, 4, 0, 2)
ES_OFF = (0, 0, 4, 4)
ES_ROWS = (48, 48, 40, 40)
ARR = 24
ZC = 2

X_PARTNERS = ((1, 0), (2, 0), (3, 0), (0, 1), (1, 1), (2, 1), (3, 1))
Y_PARTNERS = ((8, 0), (16, 0), (24, 0))
Z_PARTNERS = ((4, 0), (0, 2), (4, 2), (0, 1), (4, 1), (0, 3), (4, 3))


def pads(buf, rows):
    buf[0] = pltpu.roll(buf[rows], 1, 1)
    buf[rows + 1] = pltpu.roll(buf[1], 7, 1)


def beside(own, other, shift, edge):
    moved, moved_other = pltpu.roll(own, shift, 2), pltpu.roll(other, shift, 2)
    return jnp.where(edge, moved_other, moved), jnp.where(edge, moved, moved_other)


def zshift(buf, row, values, tile, first, last, up):
    base = tile * NZ
    if up:
        tail = values[-1:] if last == NZ else buf[row, base + last : base + last + 1]
        return jnp.concatenate([values[1:], tail], axis=0) if last - first > 1 else tail
    head = values[:1] if first == 0 else buf[row, base + first - 1 : base + first]
    return jnp.concatenate([head, values[:-1]], axis=0) if last - first > 1 else head


def neighbour_sum(cf, src, i, first, last):
    lane = lax.broadcasted_iota(jnp.int32, (last - first, 8, 128), 2)
    span = [slice(t * NZ + first, t * NZ + last) for t in (0, 1)]
    own = [src[i + 1, span[t]] for t in (0, 1)]
    south = beside(own[0], own[1], 1, lane == 0)
    north = beside(own[0], own[1], 127, lane == 127)
    sums = []
    for t in (0, 1):
        acc = cf[i, 0, span[t]] * src[i, span[t]]
        acc += cf[i, 1, span[t]] * src[i + 2, span[t]]
        acc += cf[i, 4, span[t]] * zshift(src, i + 1, own[t], t, first, last, False)
        acc += cf[i, 5, span[t]] * zshift(src, i + 1, own[t], t, first, last, True)
        acc += cf[i, 2, span[t]] * south[t]
        acc += cf[i, 3, span[t]] * north[t]
        sums.append(acc)
    return span, own, sums


def kernel(
    gxn,
    gyn,
    perm_hbm,
    stor_hbm,
    act_hbm,
    colour_hbm,
    rweight_hbm,
    sweeps,
    amap,
    source_hbm,
    sol,
    fres,
    perm,
    stor,
    act,
    colour,
    rweight,
    source,
    load,
    yp,
    pw,
    fc,
    fh,
    rw,
    raw,
    p8,
    cfs,
    ccs,
    cis,
    cols,
    rps,
    eas,
    ebs,
    ks,
    kw,
    kf,
    kfw,
    sts,
    lrs,
    lrf,
    ess,
    els,
    cls,
    idx,
    onehot,
    agg,
    ar_keep,
    ar_give,
    ar_sum,
    ar_in,
    ratio,
    wlin,
    send,
    recv,
):
    gx, gy = lax.axis_index("gx"), lax.axis_index("gy")
    core = lax.rem(gy, 2)

    def ring(dx, dy):
        return (lax.rem(gx + dx + gxn, gxn), lax.rem(gy + dy + gyn, gyn))

    def flip(dx, dy):
        return (jnp.bitwise_xor(gx, dx), jnp.bitwise_xor(gy, dy))

    counter = [0]

    def sems(n):
        counter[0] += n
        return counter[0] - n

    def copy(src, dst, sem, device):
        return pltpu.make_async_remote_copy(
            src_ref=src, dst_ref=dst, send_sem=send.at[sem], recv_sem=recv.at[sem],
            device_id=device, device_id_type=MESH,
        )

    def start(copies):
        for c in copies:
            c.start()

    def finish(copies):
        for c in copies:
            c.wait()

    barrier = pltpu.get_barrier_semaphore()
    partners = [ring(d, 0) for d in (1, -1, 2, -2, 3, -3)] + [ring(dx, dy) for dx in (-1, 0, 1) for dy in (-1, 1)]
    partners += [flip(*p) for p in X_PARTNERS + Y_PARTNERS + Z_PARTNERS]
    for device in partners:
        pl.semaphore_signal(barrier, inc=1, device_id=device, device_id_type=MESH)

    loads = [
        pltpu.make_async_copy(there, here, load.at[k])
        for k, (there, here) in enumerate(
            (
                (perm_hbm, perm), (stor_hbm, stor), (act_hbm, act), (colour_hbm, colour),
                (rweight_hbm, rweight), (source_hbm, source),
            )
        )
    ]
    start(loads)
    for l in (1, 2, 3):
        lrs[l][...] = jnp.zeros_like(lrs[l])
        els[l][...] = jnp.zeros_like(els[l])
    finish(loads)
    lane = lax.broadcasted_iota(jnp.int32, (NZ, 8, 128), 2)
    sub = lax.broadcasted_iota(jnp.int32, (NZ, 8, 128), 1)
    layer = lax.broadcasted_iota(jnp.int32, (NZ, 8, 128), 0)

    def pack(k, value):
        part = slice(k * NZ, k * NZ + NZ)
        for h in (0, 1):
            v0, v1 = value[:, 16 * h : 16 * h + 8], value[:, 16 * h + 8 : 16 * h + 16]
            a = jnp.where(sub < 4, v0, pltpu.roll(v1, 4, 1))
            b = jnp.where(sub < 4, pltpu.roll(v0, 4, 1), v1)
            rows = slice(8 * h, 8 * h + 8)
            yp[0, part, rows] = jnp.where(lane < 64, pltpu.roll(a, 64, 2), b)
            yp[1, part, rows] = jnp.where(lane < 64, a, pltpu.roll(b, 64, 2))

    def unpack(k, h, dst, at, to):
        part = slice(k * NZ, k * NZ + NZ)
        left, right = pw[0, part, 8 * h : 8 * h + 8], pw[1, part, 8 * h : 8 * h + 8]
        a = jnp.where(lane < 64, right, pltpu.roll(left, 64, 2))
        b = jnp.where(lane < 64, pltpu.roll(right, 64, 2), left)
        dst[to, at : at + 8] = jnp.where(sub < 4, a, pltpu.roll(b, 4, 1))
        dst[to, at + 8 : at + 16] = jnp.where(sub < 4, pltpu.roll(a, 4, 1), b)

    active = act[...] > 0
    for z in range(NZ):
        fc[z, 16:48] = jnp.where(active, perm[z], 0.0)
        fc[NZ + z, 16:48] = jnp.where(active, stor[z], 1.0)
        fc[2 * NZ + z, 16:48] = colour[z].astype(F32)
        fc[3 * NZ + z, 16:48] = source[z]
    for k in range(4):
        pack(k, fc[k * NZ : k * NZ + NZ, 16:48])
    pack(4, rweight[...])
    own_map = amap[...].astype(F32)
    yp[0, 50, 0:4] = own_map
    yp[1, 50, 0:4] = own_map

    RAW, RHS = slice(0, 30), slice(30, 40)
    s_y, s_xr, s_xs, s_cr, s_cs = sems(2), sems(2), sems(2), sems(4), sems(4)

    def beside_copies(v, span, raw_too):
        dy = 1 - 2 * v
        out = [copy(yp.at[v, span], pw.at[v, span, 8:24], s_y + v, ring(0, dy))]
        for q, (dx, a, to) in enumerate(((1, 12, 4), (-1, 0, 24))):
            out.append(
                copy(
                    yp.at[v, RHS, a : a + 4], pw.at[v, RHS, to : to + 4],
                    s_cs + 2 * v + q, ring(dx, dy),
                )
            )
        if raw_too:
            for q, (dx, a, to) in enumerate(((1, 8, 0), (-1, 0, 24))):
                out.append(
                    copy(
                        yp.at[v, RAW, a : a + 8], pw.at[v, RAW, to : to + 8],
                        s_cr + 2 * v + q, ring(dx, dy),
                    )
                )
        return out

    def exchange(span, raw_too, between):
        along = [
            copy(fc.at[RHS, 40:48], fc.at[RHS, 8:16], s_xs, ring(1, 0)),
            copy(fc.at[RHS, 16:24], fc.at[RHS, 48:56], s_xs + 1, ring(-1, 0)),
        ]
        if raw_too:
            along = [
                copy(fc.at[RAW, 32:48], fc.at[RAW, 0:16], s_xr, ring(1, 0)),
                copy(fc.at[RAW, 16:32], fc.at[RAW, 48:64], s_xr + 1, ring(-1, 0)),
            ] + along
        up, down = beside_copies(0, span, raw_too), beside_copies(1, span, raw_too)
        start(along)

        @pl.when(gy < gyn - 1)
        def _():
            start(up)

        @pl.when(gy > 0)
        def _():
            start(down)

        for v, edge in ((0, gy == 0), (1, gy == gyn - 1)):

            @pl.when(edge)
            def _():
                pw[v, span, 8:24] = yp[v, span]
                parts = (RAW, RHS) if raw_too else (RHS,)
                for part in parts:
                    pw[v, part, 0:8] = yp[v, part, 8:16]
                    pw[v, part, 24:32] = yp[v, part, 0:8]

        between()
        finish(along)

        @pl.when(gy < gyn - 1)
        def _():
            for c in up:
                c.wait_send()
            for c in down:
                c.wait_recv()

        @pl.when(gy > 0)
        def _():
            for c in down:
                c.wait_send()
            for c in up:
                c.wait_recv()

    def fill():
        for j in range(4):
            agg_id = lax.broadcasted_iota(jnp.int32, (NAGG, 128), 0)
            onehot[j] = (agg_id == amap[j : j + 1, :]).astype(jnp.bfloat16)
        agg[...] = jnp.zeros_like(agg)
        wlin[...] = jnp.zeros_like(wlin)
        for at, end in ((0, 8), (40, 48)):
            kw[1][:, at:end] = jnp.ones((100, end - at, 128), F32)
        for l in (2, 3):
            for _, _, _, at, end in FAR[l]:
                kw[l][0:100, at:end] = jnp.ones((100, end - at, 128), F32)
        for _, _, _, at, end in FAR[3]:
            kw[3][100:102, at:end] = jnp.zeros((2, end - at, 128), F32)
        wlin[0:NZ, 8:40] = rweight[...]
        for i in range(6):
            rw[i, 0:NZ] = wlin[0:NZ, pl.ds(i, 8, stride=6), :]

    pl.semaphore_wait(barrier, len(partners))
    exchange(slice(0, 51), True, fill)
    for k in range(4):
        for h in range(4):
            unpack(k, h, fh, 16 * h, slice(k * NZ, k * NZ + NZ))
    for h in (1, 2):
        unpack(4, h, wlin, 16 * h - 8, slice(NZ, T2))
    for i in range(6):
        rw[i, NZ:T2] = wlin[NZ:T2, pl.ds(i, 8, stride=6), :]
    mlane = lax.broadcasted_iota(jnp.int32, (4, 128), 1)
    ks[3][100, 8:12] = own_map
    ks[3][101, 8:12] = jnp.where(mlane < 64, pw[1, 50, 8:12], pw[0, 50, 8:12])

    def raw_rows(k, at, stride):
        part = slice(k * NZ, k * NZ + NZ)
        rows = pl.ds(at, 8, stride=stride)
        return jnp.concatenate([fc[part, rows, :], fh[part, rows, :]], axis=0)

    for i in range(8):
        p8[i + 1] = raw_rows(0, i, 8)
    pads(p8, 8)

    def harmonic(a, b):
        total = a + b
        return jnp.where(total > 0, 2.0 * a * b / jnp.where(total > 0, total, 1.0), 0.0)

    for m in range(4):
        pair = []
        for i in (2 * m, 2 * m + 1):
            own = [p8[i + 1, t * NZ : t * NZ + NZ] for t in (0, 1)]
            north = beside(own[0], own[1], 127, lane == 127)
            xg = gx * 32 - 16 + 8 * sub + i
            three = [[], [], []]
            for t in (0, 1):
                part = slice(t * NZ, t * NZ + NZ)
                yg = gy * 128 + lane
                if t == 1:
                    yg = jnp.where(lane < 64, yg + 128, yg - 128)
                west = harmonic(own[t], p8[i, part])
                above = 0.5 * harmonic(own[t], zshift(p8, i + 1, own[t], t, 0, NZ, True))
                three[0].append(jnp.where((xg == 0) | (xg == 1024), 0.0, west))
                three[1].append(
                    jnp.where(jnp.bitwise_and(yg, 511) == 511, 0.0, harmonic(own[t], north[t]))
                )
                three[2].append(jnp.where(layer == NZ - 1, 0.0, above))
            three = [jnp.concatenate(f, axis=0) for f in three]
            for k in range(3):
                raw[k, :, pl.ds(i, 8, stride=8), :] = three[k]
            pair.append(three)
        five = (
            raw_rows(1, 2 * m, 8) + raw_rows(1, 2 * m + 1, 8),
            pair[0][0],
            pair[0][1] + pair[1][1],
            pair[0][2] + pair[1][2],
            raw_rows(2, 2 * m, 8),
        )
        for k in range(5):
            kw[1][k * T2 : k * T2 + T2, pl.ds(8 + m, 8, stride=4), :] = five[k]

    def own_coefficients():
        for l, finer, at in ((2, kw[1], 16), (3, ks[2], 8)):
            for k in range(5):
                part = slice(k * T2, k * T2 + T2)
                value = finer[part, pl.ds(at, 8, stride=2), :]
                if k not in (1, 4):
                    value = value + finer[part, pl.ds(at + 1, 8, stride=2), :]
                ks[l][part, 8:16] = value

    def scaled(l, storage_of, west_of, north_of, above_of, colour_of):
        rows, pad = ROWS[l], eas[l]
        for i in range(rows):
            pad[i + 1] = west_of(i)
        pads(pad, rows)
        for i in range(rows):
            north, above = north_of(i), above_of(i)
            south = beside(north[0:NZ], north[NZ:T2], 1, lane == 0)
            zero = jnp.zeros((1, 8, 128), F32)
            below = [
                jnp.concatenate([zero, above[t * NZ : t * NZ + NZ - 1]], axis=0) for t in (0, 1)
            ]
            storage, shade = storage_of(i), colour_of(i)
            for t in (0, 1):
                part = slice(t * NZ, t * NZ + NZ)
                west, east = pad[i + 1, part], pad[i + 2, part]
                six = (west, east, south[t], north[part], below[t], above[part])
                centre = storage[part] + west + east + south[t] + north[part] + below[t] + above[part]
                inverse = 1.0 / centre
                for k in range(6):
                    cfs[l][i, k, part] = six[k] * inverse
                ccs[l][i, part] = centre
                cis[l][i, part] = inverse
                cols[l][i, part] = shade[part]

    def face0(k):
        return lambda i: raw[k, :, pl.ds(WS[0] + i, 8, stride=6), :]

    def raw0(k):
        return lambda i: raw_rows(k, WS[0] + i, 6)

    s_kn = [sems(len(NEAR[l])) for l in range(4)]
    s_kf = [sems(len(FAR[l])) for l in range(4)]
    s_rn = [sems(len(NEAR[l])) for l in range(4)]
    s_rf = [sems(len(FAR[l])) for l in range(4)]
    s_e = [sems(len(ITERATE[l])) for l in range(4)]
    s_ar = sems(34)
    s_kw = sems(1)

    def near_copies(l, src, own_at, dst, base, table):
        return [
            copy(src.at[:, own_at + a : own_at + b], dst.at[:, c:d], base + k, ring(right, 0))
            for k, (right, a, b, c, d) in enumerate(table)
        ]

    def far_copies(l, src, own_at, dst, base):
        return [
            copy(
                src.at[:, own_at + a : own_at + b], dst.at[k, :, c % 8 : c % 8 + 4], base + k, ring(right, 0)
            )
            for k, (right, a, b, c, d) in enumerate(FAR[l])
        ]

    def merge_far(l, far, dst):
        for k, (right, a, b, c, d) in enumerate(FAR[l]):
            dst[:, c:d] = far[k, :, c % 8 : c % 8 + 4]

    def keep_own(l, src, src_at, dst):
        n = OWN[l]
        dst[:, LO[l] : LO[l] + n] = src[:, src_at : src_at + n]
        if l == 3:
            dst[:, 28:32] = src[:, src_at : src_at + n]

    def kn_copies(l):
        if l == 2:
            return near_copies(l, ks[l], SO, kw[l], s_kn[l], NEAR[l])
        maps, base = slice(100, 102), s_kn[3]
        return near_copies(l, ks[l], SO, kw[l], base, NEAR[3][2:]) + [
            copy(ks[3].at[maps, SO : SO + 4], kw[3].at[maps, c:d], base + 2 + k, ring(right, 0))
            for k, (right, _, _, c, d) in enumerate(NEAR[3][:2])
        ]

    def nearest_blocks():
        for k in range(5):
            part = slice(k * T2, k * T2 + T2)
            for at, to in ((8, 8), (16, 12)):
                value = kw[2][part, pl.ds(at, 8, stride=2), :]
                if k not in (1, 4):
                    value = value + kw[2][part, pl.ds(at + 1, 8, stride=2), :]
                kw[3][part, to : to + 8] = value

    def kf_copies(l):
        if l > 1:
            return far_copies(l, ks[l], SO, kf[l], s_kf[l])
        west = slice(T2, 2 * T2)
        return far_copies(1, kw[1], LO[1], kf[1], s_kf[1]) + [
            copy(kw[1].at[west, 24:28], kfw.at[:, 0:4], s_kw, ring(1, 0))
        ]

    def rf_copies(l):
        return far_copies(l, sts[l], SO, lrf[l], s_rf[l])

    def level_coefficients(l):
        def pick(k):
            return lambda i: kw[l][
                k * T2 : k * T2 + T2, pl.ds(WS[l] + i, 8, stride=ROWS[l]), :
            ]

        scaled(l, pick(0), pick(1), pick(2), pick(3), pick(4))

    def half(l, src, dst, shade):
        for i in range(ROWS[l]):
            for first in range(0, NZ, ZC):
                span, own, sums = neighbour_sum(cfs[l], src, i, first, first + ZC)
                for t in (0, 1):
                    fresh = rps[l][i, span[t]] + sums[t]
                    dst[i + 1, span[t]] = jnp.where(cols[l][i, span[t]] == shade, fresh, own[t])
        pads(dst, ROWS[l])

    def left_over(l, src, i, first, last):
        span, own, sums = neighbour_sum(cfs[l], src, i, first, last)
        return span, [
            ccs[l][i, span[t]] * (rps[l][i, span[t]] + sums[t] - own[t]) for t in (0, 1)
        ]

    def before(l):
        ea, eb = eas[l], ebs[l]
        for i in range(ROWS[l]):
            if l == 0:
                scaled_rhs = raw_rows(3, WS[0] + i, 6) * cis[0][i]
            else:
                scaled_rhs = lrs[l][:, pl.ds(WS[l] + i, 8, stride=ROWS[l]), :] * cis[l][i]
            rps[l][i] = scaled_rhs
            ea[i + 1] = jnp.where(cols[l][i] == 0.0, scaled_rhs, 0.0)
        pads(ea, ROWS[l])
        half(l, ea, eb, 1.0)

        def sweep(j, carry):
            on = j < sweeps[l]
            half(l, eb, ea, jnp.where(on, 0.0, -1.0))
            half(l, ea, eb, jnp.where(on, 1.0, -1.0))
            return carry

        lax.fori_loop(1, 3, sweep, 0)

    def after(l):
        ea, eb = eas[l], ebs[l]

        def sweep(j, carry):
            on = j < sweeps[l]
            half(l, ea, eb, jnp.where(on, 0.0, -1.0))
            half(l, eb, ea, jnp.where(on, 1.0, -1.0))
            return carry

        lax.fori_loop(0, 3, sweep, 0)

    def restrict(l):
        stage, rows = sts[l + 1], ROWS[l] // 2

        for m in range(rows):
            for first in range(0, NZ, ZC):
                total = None
                for i in (2 * m, 2 * m + 1):
                    span, res = left_over(l, ebs[l], i, first, first + ZC)
                    if l == 0:
                        res = [rw[i, span[t]] * res[t] for t in (0, 1)]
                    total = res if total is None else [total[t] + res[t] for t in (0, 1)]
                for t in (0, 1):
                    stage[span[t], pl.ds(ST_OFF[l + 1] + m, 8, stride=rows), :] = total[t]

    def stage_iterate(l):
        for i in range(ROWS[l]):
            ess[l][:, pl.ds(ES_OFF[l] + i, 8, stride=ROWS[l]), :] = ebs[l][i + 1]

    def rn_copies(l):
        return near_copies(l, sts[l], SO, lrs[l], s_rn[l], NEAR[l])

    def e_copies(l):
        return near_copies(l, ess[l], ES_OFF[l] + HALO[l], els[l], s_e[l], ITERATE[l])

    def aggregate_ratio(cyc):
        s_a = s_ar + cyc * 17
        for first in range(0, NZ, ZC):
            for i in range(4):
                span, res = left_over(3, ebs[3], i, first, first + ZC)
                wlin[span[0], pl.ds(i, 8, stride=4), :] = res[0]
        for i in range(4):
            wlin[NZ:T2, pl.ds(i, 8, stride=4), :] = ccs[3][i, 0:NZ]
        total = jnp.zeros((3 * ARR, NAGG), F32)
        for i in range(4):
            for z in range(T2):
                agg[z : z + 1] = wlin[z, 12 + i : 13 + i, :]
            value = agg[...]
            high = value.astype(jnp.bfloat16)
            rest = value - high.astype(F32)
            middle = rest.astype(jnp.bfloat16)
            low = (rest - middle.astype(F32)).astype(jnp.bfloat16)
            three = jnp.concatenate([high.astype(F32), middle.astype(F32), low.astype(F32)], axis=0)
            total += lax.dot_general(
                three.astype(jnp.bfloat16), onehot[i], (((1,), (1,)), ((), ())),
                preferred_element_type=F32,
            )
        mine = total[0:ARR] + total[ARR : 2 * ARR] + total[2 * ARR :]
        low_half, high_half = mine[:, 0:256], mine[:, 256:512]
        ar_keep[...] = jnp.where(core == 0, low_half, high_half)
        ar_give[...] = jnp.where(core == 0, high_half, low_half)
        stage_iterate(3)
        at = s_a
        for stage, group in enumerate((X_PARTNERS, Y_PARTNERS, Z_PARTNERS)):
            copies = []
            for k, p in enumerate(group):
                src = ar_sum.at[stage]
                if stage == 0:
                    src = ar_give if p[1] else ar_keep
                copies.append(copy(src, ar_in.at[cyc, stage, k], at + k, flip(*p)))
            at += len(group)
            start(copies)
            if stage == 0:
                start(e_copies(3) + e_copies(2) + rf_copies(2))

                @pl.when(cyc == 0)
                def _():
                    start(kf_copies(2))

                keep_own(3, ess[3], 16, els[3])
            if stage == 2:

                @pl.when(cyc == 0)
                def _():
                    start(kf_copies(1))

            finish(copies)
            mine = ar_keep[...] if stage == 0 else ar_sum[stage]
            for k in range(7 if stage == 0 else 3):
                mine = mine + ar_in[cyc, stage, k]
            if stage < 2:
                ar_sum[stage + 1] = mine
        other = ar_in[cyc, 2, 3] + ar_in[cyc, 2, 4] + ar_in[cyc, 2, 5] + ar_in[cyc, 2, 6]
        low_half = jnp.where(core == 0, mine, other)
        high_half = jnp.where(core == 0, other, mine)
        ratio[0:NZ, 0:256] = low_half[0:NZ] / low_half[NZ:T2]
        ratio[0:NZ, 256:512] = high_half[0:NZ] / high_half[NZ:T2]

    def window_iterate(l, first):
        if l > 0:

            @pl.when(first)
            def _():
                finish(kf_copies(l))
                merge_far(l, kf[l], kw[l])
                if l == 1:
                    kw[1][T2 : 2 * T2, 8:12] = kfw[:, 0:4]
                level_coefficients(l)

            finish(rf_copies(l))
            merge_far(l, lrf[l], lrs[l])
            for i in range(ROWS[l]):
                rps[l][i] = lrs[l][:, pl.ds(WS[l] + i, 8, stride=ROWS[l]), :] * cis[l][i]
        finish(e_copies(l))
        for i in range(ROWS[l]):
            at = 0 if l == 0 else WS[l]
            now = els[l][:, pl.ds(at + i, 8, stride=ROWS[l]), :]
            if l < 3:
                at = HALO[l + 1] - HALO[l] // 2 + i // 2
                now = now + cls[l + 1][:, pl.ds(at, 8, stride=ROWS[l] // 2), :]
            eas[l][i + 1] = now

    def add_aggregates():
        def row(i, carry):
            for t in (0, 1):
                where = idx[i, t]
                place, block = jnp.bitwise_and(where, 127), jnp.right_shift(where, 7)
                for z in range(NZ):
                    value = jnp.zeros((8, 128), F32)
                    for k in range(4):
                        table = jnp.broadcast_to(
                            ratio[z : z + 1, 128 * k : 128 * k + 128], (8, 128)
                        )
                        found = jnp.take_along_axis(table, place, axis=1)
                        value = jnp.where(block == k, found, value)
                    eas[3][i + 1, t * NZ + z] += value
            return carry

        lax.fori_loop(0, 4, row, 0)

    scaled(0, raw0(1), face0(0), face0(1), face0(2), raw0(2))

    def cycle(cyc, carry):
        first = cyc == 0
        for l in range(4):
            before(l)
            if l < 3:
                restrict(l)
                start(rn_copies(l + 1))

                @pl.when(first)
                def _():
                    if l == 0:
                        own_coefficients()
                        start(kn_copies(2) + kn_copies(3))
                    if l == 2:
                        start(kf_copies(3))

                stage_iterate(l)
                if l == 1:
                    start(rf_copies(1))
                start(e_copies(l) if l < 2 else rf_copies(3))
                keep_own(l, ess[l], ES_OFF[l] + HALO[l], els[l])
                keep_own(l + 1, sts[l + 1], SO, lrs[l + 1])

                @pl.when(first)
                def _():
                    if l == 2:
                        nearest_blocks()
                    if l > 0:
                        keep_own(l + 1, ks[l + 1], SO, kw[l + 1])
                        finish(kn_copies(l + 1))
                    level_coefficients(l + 1)

                finish(rn_copies(l + 1))
        aggregate_ratio(cyc)
        for l in (3, 2, 1, 0):
            window_iterate(l, first)
            if l == 3:

                @pl.when(first)
                def _():
                    for i in range(4):
                        for t in (0, 1):
                            found = kw[3][100 + t, pl.ds(i, 8, stride=4), :]
                            idx[i, t] = found.astype(jnp.int32)

                add_aggregates()
            pads(eas[l], ROWS[l])
            after(l)
            if l > 0:
                for i in range(ROWS[l]):
                    cls[l][:, pl.ds(i, 8, stride=ROWS[l]), :] = eas[l][i + 1]

        for i in range(6):
            for z in range(0, NZ, ZC):
                span, res = left_over(0, eas[0], i, z, z + ZC)
                wlin[span[0], pl.ds(i, 8, stride=6), :] = res[0]
        leftover = wlin[0:NZ, 8:40]

        def result():
            for i in range(6):
                wlin[0:NZ, pl.ds(i, 8, stride=6), :] = eas[0][i + 1, 0:NZ]
            return wlin[0:NZ, 8:40]

        @pl.when(first)
        def _():
            fc[RHS, 16:48] = leftover
            pack(3, leftover)

            def keep():
                sol[...] = result()

            exchange(RHS, False, keep)
            for h in range(4):
                unpack(3, h, fh, 16 * h, RHS)

        @pl.when(jnp.logical_not(first))
        def _():
            fres[...] = leftover
            sol[...] += result()

        return carry

    lax.fori_loop(0, 2, cycle, 0)


def on_device(gxn, gyn, perm, stor, act, colour, rweight, sweeps, amap, source):
    def vm(*shape, dtype=F32):
        return pltpu.VMEM(shape, dtype)

    levels = range(LEVELS)
    block = perm.shape
    scratch = [
        vm(*block),
        vm(*block),
        vm(*act.shape, dtype=jnp.int32),
        vm(*block, dtype=jnp.int32),
        vm(*block),
        vm(*block),
        pltpu.SemaphoreType.DMA((6,)),
        vm(2, 51, 16, 128),
        vm(2, 51, 32, 128),
        vm(40, 64, 128),
        vm(40, 64, 128),
        vm(6, T2, 8, 128),
        vm(3, T2, 64, 128),
        vm(10, T2, 8, 128),
        [vm(ROWS[l], 6, T2, 8, 128) for l in levels],
        [vm(ROWS[l], T2, 8, 128) for l in levels],
        [vm(ROWS[l], T2, 8, 128) for l in levels],
        [vm(ROWS[l], T2, 8, 128) for l in levels],
        [vm(ROWS[l], T2, 8, 128) for l in levels],
        [vm(ROWS[l] + 2, T2, 8, 128) for l in levels],
        [vm(ROWS[l] + 2, T2, 8, 128) for l in levels],
        [vm(102 if l == 3 else 100, ST_ROWS[l], 128) for l in levels],
        [vm(102 if l == 3 else 100, LIN[l], 128) for l in levels],
        [vm(2, 102 if l == 3 else 100, 8, 128) for l in levels],
        vm(T2, 8, 128),
        [vm(T2, ST_ROWS[l], 128) for l in levels],
        [vm(T2, LIN[l], 128) for l in levels],
        [vm(2, T2, 8, 128) for l in levels],
        [vm(T2, ES_ROWS[l], 128) for l in levels],
        [vm(T2, LIN[l], 128) for l in levels],
        [vm(T2, 8 * ROWS[l], 128) for l in levels],
        vm(4, 2, 8, 128, dtype=jnp.int32),
        vm(4, NAGG, 128, dtype=jnp.bfloat16),
        vm(ARR, 128),
        vm(ARR, 256),
        vm(ARR, 256),
        vm(4, ARR, 256),
        vm(2, 3, 7, ARR, 256),
        vm(16, NAGG),
        vm(T2, 48, 128),
        pltpu.SemaphoreType.DMA((112,)),
        pltpu.SemaphoreType.DMA((112,)),
    ]
    vmem = pl.BlockSpec(memory_space=pltpu.VMEM)
    smem = pl.BlockSpec(memory_space=pltpu.SMEM)
    there = pl.BlockSpec(memory_space=pl.ANY)
    out = jax.ShapeDtypeStruct(perm.shape, F32)
    return pl.pallas_call(
        functools.partial(kernel, gxn, gyn),
        out_shape=(out, out),
        in_specs=[there, there, there, there, there, smem, vmem, there],
        out_specs=(vmem, vmem),
        scratch_shapes=scratch,
        compiler_params=pltpu.CompilerParams(
            collective_id=0, has_side_effects=True, vmem_limit_bytes=60 * 2**20
        ),
    )(perm, stor, act, colour, rweight, sweeps, amap, source)


def solution(mesh):
    field = P(None, "gx", "gy")
    column = P("gx", "gy")
    return jax.shard_map(
        functools.partial(on_device, mesh.shape["gx"], mesh.shape["gy"]),
        mesh=mesh,
        in_specs=(field, field, column, field, field, P(), column, field),
        out_specs=(field, field),
        check_vma=False,
    )
```

```python
import functools
import jax
import jax.numpy as jnp
from jax import lax
from jax.experimental import pallas as pl
from jax.experimental.pallas import tpu as pltpu
from jax.sharding import PartitionSpec as P

MESH = pl.DeviceIdType.MESH
F32 = jnp.float32
NZ = 10
T2 = 2 * NZ
LEVELS = 4
NAGG = 512
ROWS = (6, 6, 4, 4)
HALO = (8, 16, 12, 12)
OWN = (32, 16, 8, 4)
LIN = (48, 48, 40, 32)
LO = (8, 16, 16, 12)
WS = (8, 0, 4, 0)
NEAR = (
    (),
    ((1, 8, 16, 8, 16), (-1, 0, 8, 32, 40)),
    ((1, 0, 8, 8, 16), (-1, 0, 8, 24, 32)),
    ((1, 0, 4, 8, 12), (-1, 0, 4, 16, 20), (2, 0, 4, 4, 8), (-2, 0, 4, 20, 24)),
)
FAR = (
    (),
    ((1, 4, 8, 4, 8), (-1, 8, 12, 40, 44)),
    ((2, 4, 8, 4, 8), (-2, 0, 4, 32, 36)),
    ((3, 0, 4, 0, 4), (-3, 0, 4, 24, 28)),
)
ITERATE = (
    ((1, 24, 32, 0, 8), (-1, 0, 8, 40, 48)),
    ((1, 4, 16, 4, 16), (-1, 0, 12, 32, 44)),
    NEAR[2] + FAR[2],
    NEAR[3] + FAR[3],
)
SO = 8
ST_ROWS = (48, 32, 24, 24)
ST_OFF = (0, 4, 0, 2)
ES_OFF = (0, 0, 4, 4)
ES_ROWS = (48, 48, 40, 40)
ARR = 24
ZC = 2

X_PARTNERS = ((1, 0), (2, 0), (3, 0), (0, 1), (1, 1), (2, 1), (3, 1))
Y_PARTNERS = ((8, 0), (16, 0), (24, 0))
Z_PARTNERS = ((4, 0), (0, 2), (4, 2), (0, 1), (4, 1), (0, 3), (4, 3))


def pads(buf, rows):
    buf[0] = pltpu.roll(buf[rows], 1, 1)
    buf[rows + 1] = pltpu.roll(buf[1], 7, 1)


def beside(own, other, shift, edge):
    moved, moved_other = pltpu.roll(own, shift, 2), pltpu.roll(other, shift, 2)
    return jnp.where(edge, moved_other, moved), jnp.where(edge, moved, moved_other)


def zshift(buf, row, values, tile, first, last, up):
    base = tile * NZ
    if up:
        tail = values[-1:] if last == NZ else buf[row, base + last : base + last + 1]
        return jnp.concatenate([values[1:], tail], axis=0) if last - first > 1 else tail
    head = values[:1] if first == 0 else buf[row, base + first - 1 : base + first]
    return jnp.concatenate([head, values[:-1]], axis=0) if last - first > 1 else head


def neighbour_sum(cf, src, i, first, last):
    lane = lax.broadcasted_iota(jnp.int32, (last - first, 8, 128), 2)
    span = [slice(t * NZ + first, t * NZ + last) for t in (0, 1)]
    own = [src[i + 1, span[t]] for t in (0, 1)]
    south = beside(own[0], own[1], 1, lane == 0)
    north = beside(own[0], own[1], 127, lane == 127)
    sums = []
    for t in (0, 1):
        acc = cf[i, 0, span[t]] * src[i, span[t]]
        acc += cf[i, 1, span[t]] * src[i + 2, span[t]]
        acc += cf[i, 4, span[t]] * zshift(src, i + 1, own[t], t, first, last, False)
        acc += cf[i, 5, span[t]] * zshift(src, i + 1, own[t], t, first, last, True)
        acc += cf[i, 2, span[t]] * south[t]
        acc += cf[i, 3, span[t]] * north[t]
        sums.append(acc)
    return span, own, sums


def kernel(
    gxn,
    gyn,
    perm_hbm,
    stor_hbm,
    act_hbm,
    colour_hbm,
    rweight_hbm,
    sweeps,
    amap,
    source_hbm,
    sol,
    fres,
    perm,
    stor,
    act,
    colour,
    rweight,
    source,
    load,
    yp,
    pw,
    fc,
    fh,
    rw,
    raw,
    p8,
    cfs,
    ccs,
    cis,
    cols,
    rps,
    eas,
    ebs,
    ks,
    kw,
    kf,
    kfw,
    sts,
    lrs,
    lrf,
    ess,
    els,
    cls,
    idx,
    onehot,
    agg,
    ar_keep,
    ar_give,
    ar_sum,
    ar_in,
    ratio,
    wlin,
    send,
    recv,
):
    gx, gy = lax.axis_index("gx"), lax.axis_index("gy")
    core = lax.rem(gy, 2)

    def ring(dx, dy):
        return (lax.rem(gx + dx + gxn, gxn), lax.rem(gy + dy + gyn, gyn))

    def flip(dx, dy):
        return (jnp.bitwise_xor(gx, dx), jnp.bitwise_xor(gy, dy))

    counter = [0]

    def sems(n):
        counter[0] += n
        return counter[0] - n

    def copy(src, dst, sem, device):
        return pltpu.make_async_remote_copy(
            src_ref=src, dst_ref=dst, send_sem=send.at[sem], recv_sem=recv.at[sem],
            device_id=device, device_id_type=MESH,
        )

    def start(copies):
        for c in copies:
            c.start()

    def finish(copies):
        for c in copies:
            c.wait()

    barrier = pltpu.get_barrier_semaphore()
    partners = [ring(d, 0) for d in (1, -1, 2, -2, 3, -3)] + [ring(dx, dy) for dx in (-1, 0, 1) for dy in (-1, 1)]
    partners += [flip(*p) for p in X_PARTNERS + Y_PARTNERS + Z_PARTNERS]
    for device in partners:
        pl.semaphore_signal(barrier, inc=1, device_id=device, device_id_type=MESH)

    loads = [
        pltpu.make_async_copy(there, here, load.at[k])
        for k, (there, here) in enumerate(
            (
                (perm_hbm, perm), (stor_hbm, stor), (act_hbm, act), (colour_hbm, colour),
                (rweight_hbm, rweight), (source_hbm, source),
            )
        )
    ]
    start(loads)
    for l in (1, 2, 3):
        lrs[l][...] = jnp.zeros_like(lrs[l])
        els[l][...] = jnp.zeros_like(els[l])
    finish(loads)
    lane = lax.broadcasted_iota(jnp.int32, (NZ, 8, 128), 2)
    sub = lax.broadcasted_iota(jnp.int32, (NZ, 8, 128), 1)
    layer = lax.broadcasted_iota(jnp.int32, (NZ, 8, 128), 0)

    def pack(k, value):
        part = slice(k * NZ, k * NZ + NZ)
        for h in (0, 1):
            v0, v1 = value[:, 16 * h : 16 * h + 8], value[:, 16 * h + 8 : 16 * h + 16]
            a = jnp.where(sub < 4, v0, pltpu.roll(v1, 4, 1))
            b = jnp.where(sub < 4, pltpu.roll(v0, 4, 1), v1)
            rows = slice(8 * h, 8 * h + 8)
            yp[0, part, rows] = jnp.where(lane < 64, pltpu.roll(a, 64, 2), b)
            yp[1, part, rows] = jnp.where(lane < 64, a, pltpu.roll(b, 64, 2))

    def unpack(k, h, dst, at, to):
        part = slice(k * NZ, k * NZ + NZ)
        left, right = pw[0, part, 8 * h : 8 * h + 8], pw[1, part, 8 * h : 8 * h + 8]
        a = jnp.where(lane < 64, right, pltpu.roll(left, 64, 2))
        b = jnp.where(lane < 64, pltpu.roll(right, 64, 2), left)
        dst[to, at : at + 8] = jnp.where(sub < 4, a, pltpu.roll(b, 4, 1))
        dst[to, at + 8 : at + 16] = jnp.where(sub < 4, pltpu.roll(a, 4, 1), b)

    active = act[...] > 0
    for z in range(NZ):
        fc[z, 16:48] = jnp.where(active, perm[z], 0.0)
        fc[NZ + z, 16:48] = jnp.where(active, stor[z], 1.0)
        fc[2 * NZ + z, 16:48] = colour[z].astype(F32)
        fc[3 * NZ + z, 16:48] = source[z]
    for k in range(4):
        pack(k, fc[k * NZ : k * NZ + NZ, 16:48])
    pack(4, rweight[...])
    own_map = amap[...].astype(F32)
    yp[0, 50, 0:4] = own_map
    yp[1, 50, 0:4] = own_map

    RAW, RHS = slice(0, 30), slice(30, 40)
    s_y, s_xr, s_xs, s_cr, s_cs = sems(2), sems(2), sems(2), sems(4), sems(4)

    def beside_copies(v, span, raw_too):
        dy = 1 - 2 * v
        out = [copy(yp.at[v, span], pw.at[v, span, 8:24], s_y + v, ring(0, dy))]
        for q, (dx, a, to) in enumerate(((1, 12, 4), (-1, 0, 24))):
            out.append(
                copy(
                    yp.at[v, RHS, a : a + 4], pw.at[v, RHS, to : to + 4],
                    s_cs + 2 * v + q, ring(dx, dy),
                )
            )
        if raw_too:
            for q, (dx, a, to) in enumerate(((1, 8, 0), (-1, 0, 24))):
                out.append(
                    copy(
                        yp.at[v, RAW, a : a + 8], pw.at[v, RAW, to : to + 8],
                        s_cr + 2 * v + q, ring(dx, dy),
                    )
                )
        return out

    def exchange(span, raw_too, between):
        along = [
            copy(fc.at[RHS, 40:48], fc.at[RHS, 8:16], s_xs, ring(1, 0)),
            copy(fc.at[RHS, 16:24], fc.at[RHS, 48:56], s_xs + 1, ring(-1, 0)),
        ]
        if raw_too:
            along = [
                copy(fc.at[RAW, 32:48], fc.at[RAW, 0:16], s_xr, ring(1, 0)),
                copy(fc.at[RAW, 16:32], fc.at[RAW, 48:64], s_xr + 1, ring(-1, 0)),
            ] + along
        up, down = beside_copies(0, span, raw_too), beside_copies(1, span, raw_too)
        start(along)

        @pl.when(gy < gyn - 1)
        def _():
            start(up)

        @pl.when(gy > 0)
        def _():
            start(down)

        for v, edge in ((0, gy == 0), (1, gy == gyn - 1)):

            @pl.when(edge)
            def _():
                pw[v, span, 8:24] = yp[v, span]
                parts = (RAW, RHS) if raw_too else (RHS,)
                for part in parts:
                    pw[v, part, 0:8] = yp[v, part, 8:16]
                    pw[v, part, 24:32] = yp[v, part, 0:8]

        between()
        finish(along)

        @pl.when(gy < gyn - 1)
        def _():
            for c in up:
                c.wait_send()
            for c in down:
                c.wait_recv()

        @pl.when(gy > 0)
        def _():
            for c in down:
                c.wait_send()
            for c in up:
                c.wait_recv()

    def fill():
        for j in range(4):
            agg_id = lax.broadcasted_iota(jnp.int32, (NAGG, 128), 0)
            onehot[j] = (agg_id == amap[j : j + 1, :]).astype(jnp.bfloat16)
        agg[...] = jnp.zeros_like(agg)
        wlin[...] = jnp.zeros_like(wlin)
        for at, end in ((0, 8), (40, 48)):
            kw[1][:, at:end] = jnp.ones((100, end - at, 128), F32)
        for l in (2, 3):
            for _, _, _, at, end in FAR[l]:
                kw[l][0:100, at:end] = jnp.ones((100, end - at, 128), F32)
        for _, _, _, at, end in FAR[3]:
            kw[3][100:102, at:end] = jnp.zeros((2, end - at, 128), F32)
        wlin[0:NZ, 8:40] = rweight[...]
        for i in range(6):
            rw[i, 0:NZ] = wlin[0:NZ, pl.ds(i, 8, stride=6), :]

    pl.semaphore_wait(barrier, len(partners))
    exchange(slice(0, 51), True, fill)
    for k in range(4):
        for h in range(4):
            unpack(k, h, fh, 16 * h, slice(k * NZ, k * NZ + NZ))
    for h in (1, 2):
        unpack(4, h, wlin, 16 * h - 8, slice(NZ, T2))
    for i in range(6):
        rw[i, NZ:T2] = wlin[NZ:T2, pl.ds(i, 8, stride=6), :]
    mlane = lax.broadcasted_iota(jnp.int32, (4, 128), 1)
    ks[3][100, 8:12] = own_map
    ks[3][101, 8:12] = jnp.where(mlane < 64, pw[1, 50, 8:12], pw[0, 50, 8:12])

    def raw_rows(k, at, stride):
        part = slice(k * NZ, k * NZ + NZ)
        rows = pl.ds(at, 8, stride=stride)
        return jnp.concatenate([fc[part, rows, :], fh[part, rows, :]], axis=0)

    for i in range(8):
        p8[i + 1] = raw_rows(0, i, 8)
    pads(p8, 8)

    def harmonic(a, b):
        total = a + b
        return jnp.where(total > 0, 2.0 * a * b / jnp.where(total > 0, total, 1.0), 0.0)

    for m in range(4):
        pair = []
        for i in (2 * m, 2 * m + 1):
            own = [p8[i + 1, t * NZ : t * NZ + NZ] for t in (0, 1)]
            north = beside(own[0], own[1], 127, lane == 127)
            xg = gx * 32 - 16 + 8 * sub + i
            three = [[], [], []]
            for t in (0, 1):
                part = slice(t * NZ, t * NZ + NZ)
                yg = gy * 128 + lane
                if t == 1:
                    yg = jnp.where(lane < 64, yg + 128, yg - 128)
                west = harmonic(own[t], p8[i, part])
                above = 0.5 * harmonic(own[t], zshift(p8, i + 1, own[t], t, 0, NZ, True))
                three[0].append(jnp.where((xg == 0) | (xg == 1024), 0.0, west))
                three[1].append(
                    jnp.where(jnp.bitwise_and(yg, 511) == 511, 0.0, harmonic(own[t], north[t]))
                )
                three[2].append(jnp.where(layer == NZ - 1, 0.0, above))
            three = [jnp.concatenate(f, axis=0) for f in three]
            for k in range(3):
                raw[k, :, pl.ds(i, 8, stride=8), :] = three[k]
            pair.append(three)
        five = (
            raw_rows(1, 2 * m, 8) + raw_rows(1, 2 * m + 1, 8),
            pair[0][0],
            pair[0][1] + pair[1][1],
            pair[0][2] + pair[1][2],
            raw_rows(2, 2 * m, 8),
        )
        for k in range(5):
            kw[1][k * T2 : k * T2 + T2, pl.ds(8 + m, 8, stride=4), :] = five[k]

    def own_coefficients():
        for l, finer, at in ((2, kw[1], 16), (3, ks[2], 8)):
            for k in range(5):
                part = slice(k * T2, k * T2 + T2)
                value = finer[part, pl.ds(at, 8, stride=2), :]
                if k not in (1, 4):
                    value = value + finer[part, pl.ds(at + 1, 8, stride=2), :]
                ks[l][part, 8:16] = value
            if l == 2:
                start(kn_copies(2))

    def scaled(l, storage_of, west_of, north_of, above_of, colour_of):
        rows, pad = ROWS[l], eas[l]
        for i in range(rows):
            pad[i + 1] = west_of(i)
        pads(pad, rows)
        for i in range(rows):
            north, above = north_of(i), above_of(i)
            south = beside(north[0:NZ], north[NZ:T2], 1, lane == 0)
            zero = jnp.zeros((1, 8, 128), F32)
            below = [
                jnp.concatenate([zero, above[t * NZ : t * NZ + NZ - 1]], axis=0) for t in (0, 1)
            ]
            storage, shade = storage_of(i), colour_of(i)
            for t in (0, 1):
                part = slice(t * NZ, t * NZ + NZ)
                west, east = pad[i + 1, part], pad[i + 2, part]
                six = (west, east, south[t], north[part], below[t], above[part])
                centre = storage[part] + west + east + south[t] + north[part] + below[t] + above[part]
                inverse = 1.0 / centre
                for k in range(6):
                    cfs[l][i, k, part] = six[k] * inverse
                ccs[l][i, part] = centre
                cis[l][i, part] = inverse
                cols[l][i, part] = shade[part]

    def face0(k):
        return lambda i: raw[k, :, pl.ds(WS[0] + i, 8, stride=6), :]

    def raw0(k):
        return lambda i: raw_rows(k, WS[0] + i, 6)

    s_kn = [sems(len(NEAR[l])) for l in range(4)]
    s_kf = [sems(len(FAR[l])) for l in range(4)]
    s_rn = [sems(len(NEAR[l])) for l in range(4)]
    s_rf = [sems(len(FAR[l])) for l in range(4)]
    s_e = [sems(len(ITERATE[l])) for l in range(4)]
    s_ar = sems(34)
    s_kw = sems(1)

    def near_copies(l, src, own_at, dst, base, table):
        return [
            copy(src.at[:, own_at + a : own_at + b], dst.at[:, c:d], base + k, ring(right, 0))
            for k, (right, a, b, c, d) in enumerate(table)
        ]

    def far_copies(l, src, own_at, dst, base):
        return [
            copy(
                src.at[:, own_at + a : own_at + b], dst.at[k, :, c % 8 : c % 8 + 4], base + k, ring(right, 0)
            )
            for k, (right, a, b, c, d) in enumerate(FAR[l])
        ]

    def merge_far(l, far, dst):
        for k, (right, a, b, c, d) in enumerate(FAR[l]):
            dst[:, c:d] = far[k, :, c % 8 : c % 8 + 4]

    def keep_own(l, src, src_at, dst):
        n = OWN[l]
        dst[:, LO[l] : LO[l] + n] = src[:, src_at : src_at + n]
        if l == 3:
            dst[:, 28:32] = src[:, src_at : src_at + n]

    def kn_copies(l):
        if l == 2:
            return near_copies(l, ks[l], SO, kw[l], s_kn[l], NEAR[l])
        maps, base = slice(100, 102), s_kn[3]
        return near_copies(l, ks[l], SO, kw[l], base, NEAR[3][2:]) + [
            copy(ks[3].at[maps, SO : SO + 4], kw[3].at[maps, c:d], base + 2 + k, ring(right, 0))
            for k, (right, _, _, c, d) in enumerate(NEAR[3][:2])
        ]

    def nearest_blocks():
        for k in range(5):
            part = slice(k * T2, k * T2 + T2)
            for at, to in ((8, 8), (16, 12)):
                value = kw[2][part, pl.ds(at, 8, stride=2), :]
                if k not in (1, 4):
                    value = value + kw[2][part, pl.ds(at + 1, 8, stride=2), :]
                kw[3][part, to : to + 8] = value

    def kf_copies(l):
        if l > 1:
            return far_copies(l, ks[l], SO, kf[l], s_kf[l])
        west = slice(T2, 2 * T2)
        return far_copies(1, kw[1], LO[1], kf[1], s_kf[1]) + [
            copy(kw[1].at[west, 24:28], kfw.at[:, 0:4], s_kw, ring(1, 0))
        ]

    def rf_copies(l):
        return far_copies(l, sts[l], SO, lrf[l], s_rf[l])

    def level_coefficients(l):
        def pick(k):
            return lambda i: kw[l][
                k * T2 : k * T2 + T2, pl.ds(WS[l] + i, 8, stride=ROWS[l]), :
            ]

        scaled(l, pick(0), pick(1), pick(2), pick(3), pick(4))

    def half(l, src, dst, shade):
        for i in range(ROWS[l]):
            for first in range(0, NZ, ZC):
                span, own, sums = neighbour_sum(cfs[l], src, i, first, first + ZC)
                for t in (0, 1):
                    fresh = rps[l][i, span[t]] + sums[t]
                    dst[i + 1, span[t]] = jnp.where(cols[l][i, span[t]] == shade, fresh, own[t])
        pads(dst, ROWS[l])

    def left_over(l, src, i, first, last):
        span, own, sums = neighbour_sum(cfs[l], src, i, first, last)
        return span, [
            ccs[l][i, span[t]] * (rps[l][i, span[t]] + sums[t] - own[t]) for t in (0, 1)
        ]

    def before(l):
        ea, eb = eas[l], ebs[l]
        for i in range(ROWS[l]):
            if l == 0:
                scaled_rhs = raw_rows(3, WS[0] + i, 6) * cis[0][i]
            else:
                scaled_rhs = lrs[l][:, pl.ds(WS[l] + i, 8, stride=ROWS[l]), :] * cis[l][i]
            rps[l][i] = scaled_rhs
            ea[i + 1] = jnp.where(cols[l][i] == 0.0, scaled_rhs, 0.0)
        pads(ea, ROWS[l])
        half(l, ea, eb, 1.0)

        def sweep(j, carry):
            on = j < sweeps[l]
            half(l, eb, ea, jnp.where(on, 0.0, -1.0))
            half(l, ea, eb, jnp.where(on, 1.0, -1.0))
            return carry

        lax.fori_loop(1, 3, sweep, 0)

    def after(l):
        ea, eb = eas[l], ebs[l]

        def sweep(j, carry):
            on = j < sweeps[l]
            half(l, ea, eb, jnp.where(on, 0.0, -1.0))
            half(l, eb, ea, jnp.where(on, 1.0, -1.0))
            return carry

        lax.fori_loop(0, 3, sweep, 0)

    def restrict(l):
        stage, rows = sts[l + 1], ROWS[l] // 2

        for m in range(rows):
            for first in range(0, NZ, ZC):
                total = None
                for i in (2 * m, 2 * m + 1):
                    span, res = left_over(l, ebs[l], i, first, first + ZC)
                    if l == 0:
                        res = [rw[i, span[t]] * res[t] for t in (0, 1)]
                    total = res if total is None else [total[t] + res[t] for t in (0, 1)]
                for t in (0, 1):
                    stage[span[t], pl.ds(ST_OFF[l + 1] + m, 8, stride=rows), :] = total[t]

    def stage_iterate(l):
        for i in range(ROWS[l]):
            ess[l][:, pl.ds(ES_OFF[l] + i, 8, stride=ROWS[l]), :] = ebs[l][i + 1]

    def rn_copies(l):
        return near_copies(l, sts[l], SO, lrs[l], s_rn[l], NEAR[l])

    def e_copies(l):
        return near_copies(l, ess[l], ES_OFF[l] + HALO[l], els[l], s_e[l], ITERATE[l])

    def aggregate_ratio(cyc):
        s_a = s_ar + cyc * 17
        for first in range(0, NZ, ZC):
            for i in range(4):
                span, res = left_over(3, ebs[3], i, first, first + ZC)
                wlin[span[0], pl.ds(i, 8, stride=4), :] = res[0]
        for i in range(4):
            wlin[NZ:T2, pl.ds(i, 8, stride=4), :] = ccs[3][i, 0:NZ]
        total = jnp.zeros((3 * ARR, NAGG), F32)
        for i in range(4):
            for z in range(T2):
                agg[z : z + 1] = wlin[z, 12 + i : 13 + i, :]
            value = agg[...]
            high = value.astype(jnp.bfloat16)
            rest = value - high.astype(F32)
            middle = rest.astype(jnp.bfloat16)
            low = (rest - middle.astype(F32)).astype(jnp.bfloat16)
            three = jnp.concatenate([high.astype(F32), middle.astype(F32), low.astype(F32)], axis=0)
            total += lax.dot_general(
                three.astype(jnp.bfloat16), onehot[i], (((1,), (1,)), ((), ())),
                preferred_element_type=F32,
            )
        mine = total[0:ARR] + total[ARR : 2 * ARR] + total[2 * ARR :]
        low_half, high_half = mine[:, 0:256], mine[:, 256:512]
        ar_keep[...] = jnp.where(core == 0, low_half, high_half)
        ar_give[...] = jnp.where(core == 0, high_half, low_half)
        stage_iterate(3)
        at = s_a
        for stage, group in enumerate((X_PARTNERS, Y_PARTNERS, Z_PARTNERS)):
            copies = []
            for k, p in enumerate(group):
                src = ar_sum.at[stage]
                if stage == 0:
                    src = ar_give if p[1] else ar_keep
                copies.append(copy(src, ar_in.at[cyc, stage, k], at + k, flip(*p)))
            at += len(group)
            start(copies)
            if stage == 0:
                start(e_copies(3) + e_copies(2) + rf_copies(2))

                @pl.when(cyc == 0)
                def _():
                    start(kf_copies(2))

                keep_own(3, ess[3], 16, els[3])
            if stage == 2:

                @pl.when(cyc == 0)
                def _():
                    start(kf_copies(1))

            finish(copies)
            mine = ar_keep[...] if stage == 0 else ar_sum[stage]
            for k in range(7 if stage == 0 else 3):
                mine = mine + ar_in[cyc, stage, k]
            if stage < 2:
                ar_sum[stage + 1] = mine
        other = ar_in[cyc, 2, 3] + ar_in[cyc, 2, 4] + ar_in[cyc, 2, 5] + ar_in[cyc, 2, 6]
        low_half = jnp.where(core == 0, mine, other)
        high_half = jnp.where(core == 0, other, mine)
        ratio[0:NZ, 0:256] = low_half[0:NZ] / low_half[NZ:T2]
        ratio[0:NZ, 256:512] = high_half[0:NZ] / high_half[NZ:T2]

    def window_iterate(l, first):
        if l > 0:

            @pl.when(first)
            def _():
                finish(kf_copies(l))
                merge_far(l, kf[l], kw[l])
                if l == 1:
                    kw[1][T2 : 2 * T2, 8:12] = kfw[:, 0:4]
                level_coefficients(l)

            finish(rf_copies(l))
            merge_far(l, lrf[l], lrs[l])
            for i in range(ROWS[l]):
                rps[l][i] = lrs[l][:, pl.ds(WS[l] + i, 8, stride=ROWS[l]), :] * cis[l][i]
        finish(e_copies(l))
        for i in range(ROWS[l]):
            at = 0 if l == 0 else WS[l]
            now = els[l][:, pl.ds(at + i, 8, stride=ROWS[l]), :]
            if l < 3:
                at = HALO[l + 1] - HALO[l] // 2 + i // 2
                now = now + cls[l + 1][:, pl.ds(at, 8, stride=ROWS[l] // 2), :]
            eas[l][i + 1] = now

    def add_aggregates():
        def row(i, carry):
            for t in (0, 1):
                where = idx[i, t]
                place, block = jnp.bitwise_and(where, 127), jnp.right_shift(where, 7)
                for z in range(NZ):
                    value = jnp.zeros((8, 128), F32)
                    for k in range(4):
                        table = jnp.broadcast_to(
                            ratio[z : z + 1, 128 * k : 128 * k + 128], (8, 128)
                        )
                        found = jnp.take_along_axis(table, place, axis=1)
                        value = jnp.where(block == k, found, value)
                    eas[3][i + 1, t * NZ + z] += value
            return carry

        lax.fori_loop(0, 4, row, 0)

    scaled(0, raw0(1), face0(0), face0(1), face0(2), raw0(2))

    def cycle(cyc, carry):
        first = cyc == 0
        for l in range(4):
            before(l)
            if l < 3:
                restrict(l)
                start(rn_copies(l + 1))
                if l == 2:
                    start(rf_copies(3))

                @pl.when(first)
                def _():
                    if l == 0:
                        own_coefficients()
                        start(kn_copies(3))
                    if l == 2:
                        start(kf_copies(3))

                stage_iterate(l)
                if l == 1:
                    start(rf_copies(1))
                if l < 2:
                    start(e_copies(l))
                keep_own(l, ess[l], ES_OFF[l] + HALO[l], els[l])
                keep_own(l + 1, sts[l + 1], SO, lrs[l + 1])

                @pl.when(first)
                def _():
                    if l == 2:
                        nearest_blocks()
                    if l > 0:
                        keep_own(l + 1, ks[l + 1], SO, kw[l + 1])
                        finish(kn_copies(l + 1))
                    level_coefficients(l + 1)

                finish(rn_copies(l + 1))
        aggregate_ratio(cyc)
        for l in (3, 2, 1, 0):
            window_iterate(l, first)
            if l == 3:

                @pl.when(first)
                def _():
                    for i in range(4):
                        for t in (0, 1):
                            found = kw[3][100 + t, pl.ds(i, 8, stride=4), :]
                            idx[i, t] = found.astype(jnp.int32)

                add_aggregates()
            pads(eas[l], ROWS[l])
            after(l)
            if l > 0:
                for i in range(ROWS[l]):
                    cls[l][:, pl.ds(i, 8, stride=ROWS[l]), :] = eas[l][i + 1]

        for i in range(6):
            for z in range(0, NZ, ZC):
                span, res = left_over(0, eas[0], i, z, z + ZC)
                wlin[span[0], pl.ds(i, 8, stride=6), :] = res[0]
        leftover = wlin[0:NZ, 8:40]

        def result():
            for i in range(6):
                wlin[0:NZ, pl.ds(i, 8, stride=6), :] = eas[0][i + 1, 0:NZ]
            return wlin[0:NZ, 8:40]

        @pl.when(first)
        def _():
            fc[RHS, 16:48] = leftover
            pack(3, leftover)

            def keep():
                sol[...] = result()

            exchange(RHS, False, keep)
            for h in range(4):
                unpack(3, h, fh, 16 * h, RHS)

        @pl.when(jnp.logical_not(first))
        def _():
            fres[...] = leftover
            sol[...] += result()

        return carry

    lax.fori_loop(0, 2, cycle, 0)


def on_device(gxn, gyn, perm, stor, act, colour, rweight, sweeps, amap, source):
    def vm(*shape, dtype=F32):
        return pltpu.VMEM(shape, dtype)

    levels = range(LEVELS)
    block = perm.shape
    scratch = [
        vm(*block),
        vm(*block),
        vm(*act.shape, dtype=jnp.int32),
        vm(*block, dtype=jnp.int32),
        vm(*block),
        vm(*block),
        pltpu.SemaphoreType.DMA((6,)),
        vm(2, 51, 16, 128),
        vm(2, 51, 32, 128),
        vm(40, 64, 128),
        vm(40, 64, 128),
        vm(6, T2, 8, 128),
        vm(3, T2, 64, 128),
        vm(10, T2, 8, 128),
        [vm(ROWS[l], 6, T2, 8, 128) for l in levels],
        [vm(ROWS[l], T2, 8, 128) for l in levels],
        [vm(ROWS[l], T2, 8, 128) for l in levels],
        [vm(ROWS[l], T2, 8, 128) for l in levels],
        [vm(ROWS[l], T2, 8, 128) for l in levels],
        [vm(ROWS[l] + 2, T2, 8, 128) for l in levels],
        [vm(ROWS[l] + 2, T2, 8, 128) for l in levels],
        [vm(102 if l == 3 else 100, ST_ROWS[l], 128) for l in levels],
        [vm(102 if l == 3 else 100, LIN[l], 128) for l in levels],
        [vm(2, 102 if l == 3 else 100, 8, 128) for l in levels],
        vm(T2, 8, 128),
        [vm(T2, ST_ROWS[l], 128) for l in levels],
        [vm(T2, LIN[l], 128) for l in levels],
        [vm(2, T2, 8, 128) for l in levels],
        [vm(T2, ES_ROWS[l], 128) for l in levels],
        [vm(T2, LIN[l], 128) for l in levels],
        [vm(T2, 8 * ROWS[l], 128) for l in levels],
        vm(4, 2, 8, 128, dtype=jnp.int32),
        vm(4, NAGG, 128, dtype=jnp.bfloat16),
        vm(ARR, 128),
        vm(ARR, 256),
        vm(ARR, 256),
        vm(4, ARR, 256),
        vm(2, 3, 7, ARR, 256),
        vm(16, NAGG),
        vm(T2, 48, 128),
        pltpu.SemaphoreType.DMA((112,)),
        pltpu.SemaphoreType.DMA((112,)),
    ]
    vmem = pl.BlockSpec(memory_space=pltpu.VMEM)
    smem = pl.BlockSpec(memory_space=pltpu.SMEM)
    there = pl.BlockSpec(memory_space=pl.ANY)
    out = jax.ShapeDtypeStruct(perm.shape, F32)
    return pl.pallas_call(
        functools.partial(kernel, gxn, gyn),
        out_shape=(out, out),
        in_specs=[there, there, there, there, there, smem, vmem, there],
        out_specs=(vmem, vmem),
        scratch_shapes=scratch,
        compiler_params=pltpu.CompilerParams(
            collective_id=0, has_side_effects=True, vmem_limit_bytes=60 * 2**20
        ),
    )(perm, stor, act, colour, rweight, sweeps, amap, source)


def solution(mesh):
    field = P(None, "gx", "gy")
    column = P("gx", "gy")
    return jax.shard_map(
        functools.partial(on_device, mesh.shape["gx"], mesh.shape["gy"]),
        mesh=mesh,
        in_specs=(field, field, column, field, field, P(), column, field),
        out_specs=(field, field),
        check_vma=False,
    )
```
